256 devices in a mesh: wide: 32 (over z, x), grp: 8 (over y, core).
Axes of the slice: x: 4, y: 4, z: 8, core: 2. Of those that a mesh axis runs over, the one named last changes fastest.
Arguments:
- right_side: float32 [3, 2048, 16, 256], P(None, ('wide', 'grp')), may hold values from -8 to 8
- damage_bins: int32 [2048, 16, 256], P(('wide', 'grp')), may hold values from 0 to 15
Outputs:
- solution_field: float32 [3, 2048, 16, 256], P(None, ('wide', 'grp'))
The draws below stay inside these ranges and needn't reach their ends.
All inputs are finite; a program needn't handle non-finite values.
Results may differ from the reference program's by a relative error of at most 0.0001.
Values sent between devices are 32-bit elements; how exact they have to be, the bound alone decides.
A program may use at most 128 MiB of HBM per device.

```python
import math
import jax
import jax.numpy as jnp

COMP = 3
CX = 8
NY = 16
NZ = 256
NX = 2048


def smooth_load(key, noise, low_amp, high_amp):
    amp_key, comp_key = jax.random.split(key)
    blocks = NX // CX
    amplitude = jnp.exp(jax.random.uniform(amp_key, (COMP, blocks), jnp.float32, math.log(low_amp), math.log(high_amp)))
    amplitude = jnp.repeat(amplitude, CX, axis=1)
    ypos = (jnp.arange(NY, dtype=jnp.float32) + 0.5) / NY
    zpos = (jnp.arange(NZ, dtype=jnp.float32) + 0.5) / NZ
    profile = 1.0 + 0.4 * jnp.cos(math.pi * ypos)[:, None] * jnp.cos(2.0 * math.pi * zpos)[None, :]
    signs = jnp.where(jax.random.uniform(comp_key, (COMP, 1, 1, 1)) < 0.5, -1.0, 1.0)
    total = noise + signs * amplitude[:, :, None, None] * profile[None, None]
    return jnp.clip(total, -8.0, 8.0).astype(jnp.float32)


def draw_right_side(key, part):
    key = jax.random.fold_in(key, 11)
    noise_key, load_key = jax.random.split(key)
    noise = jnp.clip(jax.random.normal(noise_key, (COMP, NX, NY, NZ), jnp.float32), -4.0, 4.0)
    return smooth_load(load_key, noise, 0.5, 2.5)


def draw_damage_bins(key, part):
    key = jax.random.fold_in(key, 23)
    base_key, cell_key = jax.random.split(key)
    base = jax.random.randint(base_key, (NX // CX,), 0, 13)
    base = jnp.repeat(base, CX)
    cells = jax.random.randint(cell_key, (NX, NY, NZ), 0, 4)
    bins = jnp.clip(base[:, None, None] + cells, 0, 15).astype(jnp.int32)
    bins = bins.at[0, 0, 0].set(0)
    bins = bins.at[NX - 1, NY - 1, NZ - 1].set(15)
    return bins


def setup_inputs(seed: int = 0) -> dict:
    splits = jax.random.split(jax.random.key(seed), 3)
    return {
        "right_side": draw_right_side(jax.random.fold_in(splits[2], 71), 0),
        "damage_bins": draw_damage_bins(jax.random.fold_in(splits[2], 71), 0),
    }


mass_shift = 0.1
pre_roots = (1.15 + 0.85 * math.sqrt(0.5), 1.15 - 0.85 * math.sqrt(0.5))
post_roots = (pre_roots[1], pre_roots[0])
bottom_roots = (1.1 + 0.9 * math.cos(math.pi / 8), 1.1 - 0.9 * math.cos(math.pi / 8), 1.1 + 0.9 * math.cos(3 * math.pi / 8), 1.1 - 0.9 * math.cos(3 * math.pi / 8))

def stiffness(damage_bins):
    damage = damage_bins.astype(jnp.float32) / 16.0
    return ((1.0 - damage) ** 2 + 0.001)[None]

def harmonic(first, second):
    return 2.0 * first * second / (first + second)

def neighbours(padded):
    return [padded[:, 2:, 1:-1, 1:-1], padded[:, :-2, 1:-1, 1:-1], padded[:, 1:-1, 2:, 1:-1], padded[:, 1:-1, :-2, 1:-1], padded[:, 1:-1, 1:-1, 2:], padded[:, 1:-1, 1:-1, :-2]]

def face_terms(springs_ext, level_scale):
    padded = jnp.pad(springs_ext, ((0, 0), (0, 0), (1, 1), (1, 1)))
    center = padded[:, 1:-1, 1:-1, 1:-1]
    coeffs = [level_scale * harmonic(center, nearby) for nearby in neighbours(padded)]
    diagonal = mass_shift + coeffs[0]
    for factor in coeffs[1:]:
        diagonal = diagonal + factor
    return (diagonal, coeffs)

def operate(field, rim_fn, operator):
    diagonal, coeffs = operator
    padded = jnp.pad(rim_fn(field), ((0, 0), (0, 0), (1, 1), (1, 1)))
    result = diagonal * field
    for factor, nearby in zip(coeffs, neighbours(padded)):
        result = result - factor * nearby
    return result

def smooth(source, field, rim_fn, operator, roots):
    diagonal = operator[0]
    for inverse in roots:
        if field is None:
            field = source / (inverse * diagonal)
        else:
            field = field + (source - operate(field, rim_fn, operator)) / (inverse * diagonal)
    return field

def restrict(values):
    shape = values.shape
    blocks = values.reshape(shape[0], shape[1] // 2, 2, shape[2] // 2, 2, shape[3] // 2, 2)
    return blocks.mean(axis=(2, 4, 6))

def prolong(values):
    return jnp.repeat(jnp.repeat(jnp.repeat(values, 2, axis=1), 2, axis=2), 2, axis=3)

def padrim(field):
    return jnp.pad(field, ((0, 0), (1, 1), (0, 0), (0, 0)))

def reference(right_side, damage_bins):
    springs = stiffness(damage_bins)
    source = right_side
    stored = []
    for level_index in range(3):
        operator = face_terms(padrim(springs), 0.25 ** level_index)
        field = smooth(source, None, padrim, operator, pre_roots)
        residue = source - operate(field, padrim, operator)
        stored.append((source, field, operator))
        source = restrict(residue)
        springs = restrict(springs)
    operator = face_terms(padrim(springs), 0.25 ** 3)
    field = smooth(source, None, padrim, operator, bottom_roots)
    for level_index in (2, 1, 0):
        source, coarse_start, operator = stored[level_index]
        field = coarse_start + prolong(field)
        field = smooth(source, field, padrim, operator, post_roots)
    return field
```

```python
import functools
import math

import jax
import jax.numpy as jnp
from jax import lax
from jax.experimental import pallas as pl
from jax.experimental.pallas import tpu as pltpu
from jax.sharding import PartitionSpec as P

MESH = pl.DeviceIdType.MESH
F32 = jnp.float32

mass_shift = 0.1
root_a = 1.15 + 0.85 * math.sqrt(0.5)
root_b = 1.15 - 0.85 * math.sqrt(0.5)
bottom_roots = (
    1.1 + 0.9 * math.cos(math.pi / 8),
    1.1 - 0.9 * math.cos(math.pi / 8),
    1.1 + 0.9 * math.cos(3 * math.pi / 8),
    1.1 - 0.9 * math.cos(3 * math.pi / 8),
)

D_UP, D_DN, B_UP, B_DN, K1_UP, K1_DN, B1_UP, B1_DN, X1_UP, X1_DN, X0_UP, X0_DN = range(12)
K2_FIRST = 12
B2_FIRST = 26
REMOTE = 38
REACH_K, REACH_B = 7, 6


def inverse(x):
    guess = pltpu.reciprocal(x, approx=True)
    return guess * (2.0 - x * guess)


def harmonic(first, second, scale):
    return (2.0 * scale) * (first * second) * inverse(first + second)


def gather(x, index, axis):
    return jnp.take_along_axis(x, index, axis=axis, mode="promise_in_bounds")


def rolled(x, shift, axis):
    return pltpu.roll(x, shift % x.shape[axis], axis)


def planar_faces(k, scale, hop, row_end, lane_end):
    axis = k.ndim - 2
    rows_up = jnp.where(row_end, 0.0, harmonic(k, rolled(k, -hop, axis), scale))
    lanes_up = jnp.where(lane_end, 0.0, harmonic(k, rolled(k, -hop, axis + 1), scale))
    return rows_up, rolled(rows_up, hop, axis), lanes_up, rolled(lanes_up, hop, axis + 1)


def residue(b, v, before, after, c, hop):
    axis = v.ndim - 2
    first = (b - c[6] * v) + (c[0] * before + c[1] * after)
    second = c[2] * rolled(v, -hop, axis) + c[3] * rolled(v, hop, axis)
    third = c[4] * rolled(v, -hop, axis + 1) + c[5] * rolled(v, hop, axis + 1)
    return first + (second + third)


def kernel(n, wide, grp, load_ref, bins_ref, out_ref, d_buf, b_buf, k_buf, cx, cyu, cyd, czu, czd, dg, da, db,
           v_buf, x_buf, s_buf, t_buf, o_buf, tmp, b1, k1, x1, c1x, c1, b2, k2, c2x, c2, c3x, c3,
           send, recv, local):
    p = lax.axis_index("wide") * grp + lax.axis_index("grp")

    def place(distance):
        q = lax.rem(p + (distance + n), n)
        return {"wide": lax.div(q, grp), "grp": lax.rem(q, grp)}

    def message(src, dst, number, distance):
        return pltpu.make_async_remote_copy(
            src_ref=src, dst_ref=dst, send_sem=send.at[number], recv_sem=recv.at[number],
            device_id=place(distance), device_id_type=MESH)

    d_up = message(bins_ref.at[5:8], d_buf.at[0:3], D_UP, 1)
    d_dn = message(bins_ref.at[0:3], d_buf.at[11:14], D_DN, -1)
    b_up = message(load_ref.at[:, 6:8], b_buf.at[:, 0:2], B_UP, 1)
    b_dn = message(load_ref.at[:, 0:2], b_buf.at[:, 10:12], B_DN, -1)
    k1_up = message(k1.at[4:7], k1.at[0:3], K1_UP, 1)
    k1_dn = message(k1.at[3:6], k1.at[7:10], K1_DN, -1)
    b1_up = message(b1.at[:, 4:6], b1.at[:, 0:2], B1_UP, 1)
    b1_dn = message(b1.at[:, 2:4], b1.at[:, 6:8], B1_DN, -1)
    x1_up = message(x1.at[:, 4:6], x1.at[:, 0:2], X1_UP, 1)
    x1_dn = message(x1.at[:, 4:6], x1.at[:, 8:10], X1_DN, -1)
    x0_up = message(x_buf.at[:, 8], x_buf.at[:, 0], X0_UP, 1)
    x0_dn = message(x_buf.at[:, 3], x_buf.at[:, 11], X0_DN, -1)
    k2_all, b2_all = [], []
    for reach, buf, first, group in ((REACH_K, k2, K2_FIRST, k2_all), (REACH_B, b2, B2_FIRST, b2_all)):
        for step in range(1, reach + 1):
            for side, distance in enumerate((step, -step)):
                spot = 14 - 2 * distance
                group.append(message(buf.at[14:16], buf.at[spot:spot + 2], first + 2 * (step - 1) + side, distance))

    bins_in = pltpu.make_async_copy(bins_ref, d_buf.at[3:11], local.at[0])
    load_in = pltpu.make_async_copy(load_ref, b_buf.at[:, 2:10], local.at[1])
    bins_in.start()
    load_in.start()
    barrier = pltpu.get_barrier_semaphore()
    for step in range(1, REACH_K + 1):
        for distance in (step, -step):
            pl.semaphore_signal(barrier, inc=1, device_id=place(distance), device_id_type=MESH)

    row0 = lax.broadcasted_iota(jnp.int32, (16, 256), 0)
    lane0 = lax.broadcasted_iota(jnp.int32, (16, 256), 1)
    row = lax.broadcasted_iota(jnp.int32, (8, 128), 0)
    lane = lax.broadcasted_iota(jnp.int32, (8, 128), 1)

    def planes(first, last, body):
        for j in range(first, last):
            body(j)

    def halve_lanes(low, high):
        even, odd = (2 * lane) & 127, (2 * lane + 1) & 127
        return jnp.where(lane < 64, gather(low, even, 1) + gather(low, odd, 1), gather(high, even, 1) + gather(high, odd, 1))

    def halve_fine(x, slot):
        tmp[slot, 0] = x[:, :128]
        tmp[slot, 1] = x[:, 128:]
        parts = [tmp[slot, h, pl.ds(0, 8, stride=2), :] + tmp[slot, h, pl.ds(1, 8, stride=2), :] for h in (0, 1)]
        return halve_lanes(parts[0], parts[1])

    def halve_middle(x):
        x = gather(x, (2 * lane) & 127, 1) + gather(x, (2 * lane + 1) & 127, 1)
        return gather(x, (2 * row) & 7, 0) + gather(x, (2 * row + 1) & 7, 0)

    bins_in.wait()

    def own_k(j):
        k_buf[j] = (1.0 - d_buf[j].astype(F32) * 0.0625) ** 2 + 0.001

    planes(3, 11, own_k)
    for j in range(4):
        k1[3 + j] = 0.125 * halve_fine(k_buf[3 + 2 * j] + k_buf[4 + 2 * j], j)
    for j in range(2):
        k2[14 + j] = 0.125 * halve_middle(k1[3 + 2 * j] + k1[4 + 2 * j])

    pl.semaphore_wait(barrier, 2 * REACH_K)
    for m in (d_up, d_dn, b_up, b_dn, k1_up, k1_dn, *k2_all):
        m.start()

    edges = (2 - 8 * p, 2 + 8 * (n - p))

    def x_face(f):
        inside = jnp.where(jnp.logical_or(f == edges[0], f == edges[1]), 0.0, 1.0)
        cx[f] = harmonic(k_buf[f], k_buf[f + 1], 1.0) * inside

    def yz_faces(j):
        cyu[j], cyd[j], czu[j], czd[j] = planar_faces(k_buf[j + 1], 1.0, 1, row0 == 15, lane0 == 255)

    def diagonal(j):
        total = (mass_shift + (cx[j] + cx[j + 1])) + ((cyu[j] + cyd[j]) + (czu[j] + czd[j]))
        dg[j] = total
        inv = inverse(total)
        da[j] = inv * (1.0 / root_a)
        db[j] = inv * (1.0 / root_b)

    def first_v(j):
        for c in range(3):
            v_buf[c, j] = b_buf[c, j] * da[j]

    def fine_residue(ref, c, j, at):
        coeffs = (cx[j], cx[j + 1], cyu[j], cyd[j], czu[j], czd[j], dg[j])
        return residue(b_buf[c, j], ref[c, at], ref[c, at - 1], ref[c, at + 1], coeffs, 1)

    def second_v(j):
        for c in range(3):
            x_buf[c, j] = v_buf[c, j] + fine_residue(v_buf, c, j, j) * db[j]

    planes(3, 10, x_face)
    planes(2, 10, yz_faces)
    planes(3, 9, diagonal)
    load_in.wait()
    planes(3, 9, first_v)
    planes(4, 8, second_v)

    d_up.wait_recv()
    d_dn.wait_recv()
    for j in (0, 1, 2, 11, 12, 13):
        own_k(j)
    for f in (0, 1, 2, 10, 11, 12):
        x_face(f)
    for j in (0, 1, 10, 11):
        yz_faces(j)
    for j in (0, 1, 2, 9, 10, 11):
        diagonal(j)
    b_up.wait_recv()
    b_dn.wait_recv()
    for j in (0, 1, 2, 9, 10, 11):
        first_v(j)
    for j in (1, 2, 3, 8, 9, 10):
        second_v(j)
    for j in range(4):
        for c in range(3):
            both = fine_residue(x_buf, c, 2 * j + 2, 2 * j + 2) + fine_residue(x_buf, c, 2 * j + 3, 2 * j + 3)
            b1[c, 2 + j] = 0.125 * halve_fine(both, 4 + 3 * j + c)
    for m in (b1_up, b1_dn, x0_up, x0_dn):
        m.start()

    def edge_mask(count, spot, each):
        face = lax.broadcasted_iota(jnp.int32, (count, 8, 128), 0)
        return jnp.logical_or(face == spot - each * p, face == spot + each * (n - p))

    def level(k_x, k_yz, count, spot, each, scale, hop, row_end, lane_end, x_ref, ref):
        x_ref[...] = jnp.where(edge_mask(count + 1, spot, each), 0.0, harmonic(k_x[:-1], k_x[1:], scale))
        faces = planar_faces(k_yz, scale, hop, row_end, lane_end)
        for i, face in enumerate(faces):
            ref[i] = face
        total = (mass_shift + (x_ref[:-1] + x_ref[1:])) + ((faces[0] + faces[1]) + (faces[2] + faces[3]))
        ref[4] = total
        ref[5] = inverse(total)

    def apply(b, v, x_ref, ref, hop, first, last):
        inner = slice(first, last)
        coeffs = (x_ref[inner], x_ref[first + 1:last + 1], ref[0, inner], ref[1, inner], ref[2, inner], ref[3, inner], ref[4, inner])
        return residue(b, v[1:-1], v[:-2], v[2:], coeffs, hop)

    k1_up.wait_recv()
    k1_dn.wait_recv()
    level(k1[...], k1[1:9], 8, 2, 4, 0.25, 1, (row == 7)[None], (lane == 127)[None], c1x, c1)

    for m in k2_all:
        m.wait_recv()
    level(k2[1:29], k2[2:28], 26, 12, 2, 0.25 ** 2, 1, ((row & 3) == 3)[None], ((lane & 63) == 63)[None], c2x, c2)

    def halve_coarse(x):
        pairs = x.reshape(x.shape[0] // 2, 2, 8, 128)
        x = pairs[:, 0] + pairs[:, 1]
        x = x + gather(x, jnp.broadcast_to((row ^ 1)[None], x.shape), 1)
        return 0.125 * (x + gather(x, jnp.broadcast_to((lane ^ 1)[None], x.shape), 2))

    k3 = halve_coarse(k2[2:28])
    level(k3, k3[1:-1], 11, 5, 1, 0.25 ** 3, 2, ((row & 3) >= 2)[None], ((lane & 63) >= 62)[None], c3x, c3)

    b1_up.wait_recv()
    b1_dn.wait_recv()
    rest = []
    for c in range(3):
        v = b1[c] * (c1[5] * (1.0 / root_a))
        x = v[1:-1] + apply(b1[c, 1:7], v, c1x, c1, 1, 1, 7) * (c1[5, 1:7] * (1.0 / root_b))
        x1[c, 2:8] = x
        r = apply(b1[c, 2:6], x, c1x, c1, 1, 2, 6)
        rest.append(r)
    quarter = (row >= 4).astype(jnp.int32) * 2 + (lane >= 64).astype(jnp.int32)
    for j in range(2):
        parts = [halve_middle(r[2 * j] + r[2 * j + 1]) for r in rest]
        b2[14 + j] = 0.125 * jnp.where(quarter == 0, parts[0], jnp.where(quarter == 1, parts[1], parts[2]))
    for m in b2_all:
        m.start()
    x1_up.start()
    x1_dn.start()

    for m in b2_all:
        m.wait_recv()
    v = b2[2:28] * (c2[5] * (1.0 / root_a))
    x = v[1:-1] + apply(b2[3:27], v, c2x, c2, 1, 1, 25) * (c2[5, 1:25] * (1.0 / root_b))
    r = apply(b2[4:26], x, c2x, c2, 1, 2, 24)
    b3 = halve_coarse(r)
    low = b3 * (c3[5] * (1.0 / bottom_roots[0]))
    for i in (1, 2, 3):
        inner = slice(i, 11 - i)
        low = low[1:-1] + apply(b3[inner], low, c3x, c3, 2, i, 11 - i) * (c3[5, inner] * (1.0 / bottom_roots[i]))
    v = x[7:17] + jnp.broadcast_to(low[:, None], (5, 2, 8, 128)).reshape(10, 8, 128)
    v = v[1:-1] + apply(b2[11:19], v, c2x, c2, 1, 9, 17) * (c2[5, 9:17] * (1.0 / root_b))
    x = v[1:-1] + apply(b2[12:18], v, c2x, c2, 1, 10, 16) * (c2[5, 10:16] * (1.0 / root_a))

    x1_up.wait_recv()
    x1_dn.wait_recv()
    ups = []
    for c in range(3):
        spread = []
        for j in range(6):
            part = gather(x[j], 64 * (c % 2) + (lane >> 1), 1)
            spread.append(gather(part, 4 * (c // 2) + (row >> 1), 0))
        v = jnp.stack([x1[c, i] + spread[(i + 1) // 2] for i in range(10)])
        v = v[1:-1] + apply(b1[c], v, c1x, c1, 1, 0, 8) * (c1[5] * (1.0 / root_b))
        ups.append(v[1:-1] + apply(b1[c, 1:7], v, c1x, c1, 1, 1, 7) * (c1[5, 1:7] * (1.0 / root_a)))

    x0_up.wait_recv()
    x0_dn.wait_recv()
    for j in range(6):
        for c in range(3):
            spread = []
            for h in range(2):
                part = gather(ups[c][j], 64 * h + (lane >> 1), 1)
                spread.append(jnp.concatenate([gather(part, row >> 1, 0), gather(part, 4 + (row >> 1), 0)], axis=0))
            spread = jnp.concatenate(spread, axis=1)
            for i in (2 * j, 2 * j + 1):
                s_buf[c, i] = x_buf[c, i] + spread
    for j in range(1, 11):
        for c in range(3):
            t_buf[c, j - 1] = s_buf[c, j] + fine_residue(s_buf, c, j, j) * db[j]
    for j in range(2, 10):
        for c in range(3):
            o_buf[c, j - 2] = t_buf[c, j - 1] + fine_residue(t_buf, c, j, j - 1) * da[j]
    out = pltpu.make_async_copy(o_buf, out_ref, local.at[2])
    out.start()
    for m in (d_up, d_dn, b_up, b_dn, k1_up, k1_dn, b1_up, b1_dn, x1_up, x1_dn, x0_up, x0_dn, *k2_all, *b2_all):
        m.wait_send()
    out.wait()


def solution(mesh):
    wide, grp = mesh.shape["wide"], mesh.shape["grp"]

    def on_device(load, bins):
        def plane(*lead):
            return pltpu.VMEM((*lead, 16, 256), F32)

        def small(*lead):
            return pltpu.VMEM((*lead, 8, 128), F32)

        return pl.pallas_call(
            functools.partial(kernel, wide * grp, wide, grp),
            out_shape=jax.ShapeDtypeStruct(load.shape, F32),
            in_specs=[pl.BlockSpec(memory_space=pl.ANY)] * 2,
            out_specs=pl.BlockSpec(memory_space=pl.ANY),
            scratch_shapes=[
                pltpu.VMEM((14, 16, 256), jnp.int32), plane(3, 12), plane(14), plane(13),
                *[plane(12) for _ in range(7)],
                plane(3, 12), plane(3, 12), plane(3, 12), plane(3, 10), plane(3, 8),
                pltpu.VMEM((16, 2, 16, 128), F32),
                small(3, 8), small(10), small(3, 10), small(9), small(6, 8),
                small(30), small(30), small(27), small(6, 26), small(12), small(6, 11),
                pltpu.SemaphoreType.DMA((REMOTE,)), pltpu.SemaphoreType.DMA((REMOTE,)), pltpu.SemaphoreType.DMA((3,)),
            ],
            compiler_params=pltpu.CompilerParams(
                collective_id=0, has_side_effects=True, vmem_limit_bytes=40 * 1024 * 1024),
        )(load, bins)

    return jax.shard_map(
        on_device,
        mesh=mesh,
        in_specs=(P(None, ("wide", "grp"), None, None), P(("wide", "grp"), None, None)),
        out_specs=P(None, ("wide", "grp"), None, None),
        check_vma=False,
    )
```

```python
import functools
import math

import jax
import jax.numpy as jnp
from jax import lax
from jax.experimental import pallas as pl
from jax.experimental.pallas import tpu as pltpu
from jax.sharding import PartitionSpec as P

MESH = pl.DeviceIdType.MESH
F32 = jnp.float32

mass_shift = 0.1
root_a = 1.15 + 0.85 * math.sqrt(0.5)
root_b = 1.15 - 0.85 * math.sqrt(0.5)
bottom_roots = (
    1.1 + 0.9 * math.cos(math.pi / 8),
    1.1 - 0.9 * math.cos(math.pi / 8),
    1.1 + 0.9 * math.cos(3 * math.pi / 8),
    1.1 - 0.9 * math.cos(3 * math.pi / 8),
)

D_UP, D_DN, B_UP, B_DN, K1_UP, K1_DN, K1_FAR_UP, K1_FAR_DN, B1_UP, B1_DN, X0_UP, X0_DN = range(12)
K2_FIRST = 12
M2_FIRST = 24
M3_FIRST = 30
REMOTE = 44
REACH_K, REACH_2, REACH_3 = 6, 3, 7


def inverse(x):
    guess = pltpu.reciprocal(x, approx=True)
    return guess * (2.0 - x * guess)


def harmonic(first, second, scale):
    return (2.0 * scale) * (first * second) * inverse(first + second)


def gather(x, index, axis):
    return jnp.take_along_axis(x, index, axis=axis, mode="promise_in_bounds")


def rolled(x, shift, axis):
    return pltpu.roll(x, shift % x.shape[axis], axis)


def planar_faces(k, scale, hop, row_end, lane_end):
    axis = k.ndim - 2
    rows_up = jnp.where(row_end, 0.0, harmonic(k, rolled(k, -hop, axis), scale))
    lanes_up = jnp.where(lane_end, 0.0, harmonic(k, rolled(k, -hop, axis + 1), scale))
    return rows_up, rolled(rows_up, hop, axis), lanes_up, rolled(lanes_up, hop, axis + 1)


def residue(b, v, before, after, c, hop):
    axis = v.ndim - 2
    first = (b - c[6] * v) + (c[0] * before + c[1] * after)
    second = c[2] * rolled(v, -hop, axis) + c[3] * rolled(v, hop, axis)
    third = c[4] * rolled(v, -hop, axis + 1) + c[5] * rolled(v, hop, axis + 1)
    return first + (second + third)


def kernel(n, wide, grp, load_ref, bins_ref, out_ref, d_buf, b_buf, k_buf, cx, cyu, cyd, czu, czd, dg, da, db,
           v_buf, x_buf, s_buf, t_buf, tmp, b1, k1, c1x, c1, k2, m2, c2x, c2, m3, c3x, c3, send, recv, local):
    p = lax.axis_index("wide") * grp + lax.axis_index("grp")

    def place(distance):
        q = lax.rem(p + (distance + n), n)
        return {"wide": lax.div(q, grp), "grp": lax.rem(q, grp)}

    def there(distance):
        return p + distance < n if distance > 0 else p + distance >= 0

    class Message:
        def __init__(self, src, dst, number, distance):
            self.distance = distance
            self.copy = pltpu.make_async_remote_copy(
                src_ref=src, dst_ref=dst, send_sem=send.at[number], recv_sem=recv.at[number],
                device_id=place(distance), device_id_type=MESH)

        def start(self):
            pl.when(there(self.distance))(self.copy.start)

        def wait_send(self):
            pl.when(there(self.distance))(self.copy.wait_send)

        def wait_recv(self):
            pl.when(there(-self.distance))(self.copy.wait_recv)

    def both_ways(reach):
        return [d for step in range(1, reach + 1) for d in (step, -step)]

    d_up = Message(bins_ref.at[5:8], d_buf.at[0:3], D_UP, 1)
    d_dn = Message(bins_ref.at[0:3], d_buf.at[11:14], D_DN, -1)
    b_up = Message(load_ref.at[:, 6:8], b_buf.at[:, 0:2], B_UP, 1)
    b_dn = Message(load_ref.at[:, 0:2], b_buf.at[:, 10:12], B_DN, -1)
    k1_up = Message(k1.at[5:9], k1.at[1:5], K1_UP, 1)
    k1_dn = Message(k1.at[5:9], k1.at[9:13], K1_DN, -1)
    k1_far_up = Message(k1.at[8], k1.at[0], K1_FAR_UP, 2)
    k1_far_dn = Message(k1.at[5], k1.at[13], K1_FAR_DN, -2)
    b1_up = Message(b1.at[:, 4:8], b1.at[:, 0:4], B1_UP, 1)
    b1_dn = Message(b1.at[:, 4:8], b1.at[:, 8:12], B1_DN, -1)
    x0_up = Message(x_buf.at[:, 8], x_buf.at[:, 0], X0_UP, 1)
    x0_dn = Message(x_buf.at[:, 3], x_buf.at[:, 11], X0_DN, -1)
    k2_all = [Message(k2.at[12:14], k2.at[12 - 2 * d:14 - 2 * d], K2_FIRST + i, d) for i, d in enumerate(both_ways(REACH_K))]
    part = {3: slice(2, 4), -3: slice(0, 2)}
    m2_all = [Message(m2.at[3, part.get(d, slice(0, 4))], m2.at[3 - d, part.get(d, slice(0, 4))], M2_FIRST + i, d)
              for i, d in enumerate(both_ways(REACH_2))]
    m3_all = [Message(m3.at[7], m3.at[7 - d], M3_FIRST + i, d) for i, d in enumerate(both_ways(REACH_3))]
    all_messages = [d_up, d_dn, b_up, b_dn, k1_up, k1_dn, k1_far_up, k1_far_dn, b1_up, b1_dn, x0_up, x0_dn,
                    *k2_all, *m2_all, *m3_all]

    @pl.when(jnp.logical_or(p < REACH_3, p >= n - REACH_3))
    def _():
        for halo in (slice(0, 3), slice(11, 14)):
            d_buf[halo] = jnp.zeros((3, 16, 256), jnp.int32)
        for halo in (slice(0, 2), slice(10, 12)):
            b_buf[:, halo] = jnp.zeros((3, 2, 16, 256), F32)
        for j in (0, 11):
            x_buf[:, j] = jnp.zeros((3, 16, 256), F32)
        k1[...] = jnp.ones_like(k1)
        b1[...] = jnp.zeros_like(b1)
        k2[...] = jnp.ones_like(k2)
        m2[...] = jnp.zeros_like(m2)
        m3[...] = jnp.zeros_like(m3)

    bins_in = pltpu.make_async_copy(bins_ref, d_buf.at[3:11], local.at[0])
    load_in = pltpu.make_async_copy(load_ref, b_buf.at[:, 2:10], local.at[1])
    bins_in.start()
    load_in.start()
    barrier = pltpu.get_barrier_semaphore()
    for d in both_ways(REACH_3):
        pl.when(there(d))(functools.partial(
            pl.semaphore_signal, barrier, inc=1, device_id=place(d), device_id_type=MESH))

    row0 = lax.broadcasted_iota(jnp.int32, (16, 256), 0)
    lane0 = lax.broadcasted_iota(jnp.int32, (16, 256), 1)
    row = lax.broadcasted_iota(jnp.int32, (8, 128), 0)
    lane = lax.broadcasted_iota(jnp.int32, (8, 128), 1)

    def planes(first, last, body):
        for j in range(first, last):
            body(j)

    def halve_lanes(low, high):
        even, odd = (2 * lane) & 127, (2 * lane + 1) & 127
        return jnp.where(lane < 64, gather(low, even, 1) + gather(low, odd, 1), gather(high, even, 1) + gather(high, odd, 1))

    def halve_fine(x, slot):
        tmp[slot, 0] = x[:, :128]
        tmp[slot, 1] = x[:, 128:]
        parts = [tmp[slot, h, pl.ds(0, 8, stride=2), :] + tmp[slot, h, pl.ds(1, 8, stride=2), :] for h in (0, 1)]
        return halve_lanes(parts[0], parts[1])

    def halve_middle(x):
        x = gather(x, (2 * lane) & 127, 1) + gather(x, (2 * lane + 1) & 127, 1)
        return gather(x, (2 * row) & 7, 0) + gather(x, (2 * row + 1) & 7, 0)

    bins_in.wait()

    def own_k(j):
        k_buf[j] = (1.0 - d_buf[j].astype(F32) * 0.0625) ** 2 + 0.001

    planes(3, 11, own_k)
    for j in range(4):
        k1[5 + j] = 0.125 * halve_fine(k_buf[3 + 2 * j] + k_buf[4 + 2 * j], j)
    for j in range(2):
        k2[12 + j] = 0.125 * halve_middle(k1[5 + 2 * j] + k1[6 + 2 * j])

    pl.semaphore_wait(barrier, jnp.minimum(p, REACH_3) + jnp.minimum(n - 1 - p, REACH_3))
    for m in (d_up, d_dn, k1_up, k1_dn, *k2_all[:6], k1_far_up, k1_far_dn, b_up, b_dn, *k2_all[6:]):
        m.start()

    edges = (2 - 8 * p, 2 + 8 * (n - p))

    def x_face(f):
        inside = jnp.where(jnp.logical_or(f == edges[0], f == edges[1]), 0.0, 1.0)
        cx[f] = harmonic(k_buf[f], k_buf[f + 1], 1.0) * inside

    def yz_faces(j):
        cyu[j], cyd[j], czu[j], czd[j] = planar_faces(k_buf[j + 1], 1.0, 1, row0 == 15, lane0 == 255)

    def diagonal(j):
        total = (mass_shift + (cx[j] + cx[j + 1])) + ((cyu[j] + cyd[j]) + (czu[j] + czd[j]))
        dg[j] = total
        inv = inverse(total)
        da[j] = inv * (1.0 / root_a)
        db[j] = inv * (1.0 / root_b)

    def first_v(j):
        for c in range(3):
            v_buf[c, j] = b_buf[c, j] * da[j]

    def fine_residue(ref, c, j, at):
        coeffs = (cx[j], cx[j + 1], cyu[j], cyd[j], czu[j], czd[j], dg[j])
        return residue(b_buf[c, j], ref[c, at], ref[c, at - 1], ref[c, at + 1], coeffs, 1)

    def second_v(j):
        for c in range(3):
            x_buf[c, j] = v_buf[c, j] + fine_residue(v_buf, c, j, j) * db[j]

    planes(3, 10, x_face)
    planes(2, 10, yz_faces)
    planes(3, 9, diagonal)
    load_in.wait()
    planes(3, 9, first_v)
    planes(4, 8, second_v)

    d_up.wait_recv()
    d_dn.wait_recv()
    for j in (0, 1, 2, 11, 12, 13):
        own_k(j)
    for f in (0, 1, 2, 10, 11, 12):
        x_face(f)
    for j in (0, 1, 10, 11):
        yz_faces(j)
    for j in (0, 1, 2, 9, 10, 11):
        diagonal(j)
    def edge_mask(count, spot, each):
        face = lax.broadcasted_iota(jnp.int32, (count, 8, 128), 0)
        return jnp.logical_or(face == spot - each * p, face == spot + each * (n - p))

    def level(k, count, spot, each, scale, hop, row_end, lane_end, x_ref, ref):
        x_ref[...] = jnp.where(edge_mask(count + 1, spot, each), 0.0, harmonic(k[:-1], k[1:], scale))
        faces = planar_faces(k[1:-1], scale, hop, row_end, lane_end)
        for i, face in enumerate(faces):
            ref[i] = face
        total = (mass_shift + (x_ref[:-1] + x_ref[1:])) + ((faces[0] + faces[1]) + (faces[2] + faces[3]))
        ref[4] = total
        inv = inverse(total)
        ref[5] = inv
        ref[6] = inv * (1.0 / root_a)
        ref[7] = inv * (1.0 / root_b)

    def apply(b, v, x_ref, ref, hop, first, last):
        inner = slice(first, last)
        coeffs = (x_ref[inner], x_ref[first + 1:last + 1], ref[0, inner], ref[1, inner], ref[2, inner], ref[3, inner], ref[4, inner])
        return residue(b, v[1:-1], v[:-2], v[2:], coeffs, hop)

    def widen(x, by):
        none = jnp.zeros((by, 8, 128), F32)
        return jnp.concatenate([none, x, none], axis=0)

    def pre_smooth(b, x_ref, ref):
        v = b * ref[6]
        return v[1:-1] + apply(b[1:-1], v, x_ref, ref, 1, 1, 11) * ref[7, 1:11]

    def post_smooth(b, start, x_ref, ref):
        v = start[1:-1] + apply(b[2:10], start, x_ref, ref, 1, 2, 10) * ref[7, 2:10]
        return v[1:-1] + apply(b[3:9], v, x_ref, ref, 1, 3, 9) * ref[6, 3:9]

    def share(b, x_ref, ref):
        v = widen(b * ref[6, 4:8], 2)
        x = widen(v[1:-1] + apply(widen(b, 1), v, x_ref, ref, 1, 3, 9) * ref[7, 3:9], 2)
        return apply(widen(b, 2), x, x_ref, ref, 1, 2, 10)

    for m in (k1_up, k1_dn, k1_far_up, k1_far_dn):
        m.wait_recv()
    level(k1[...], 12, 4, 4, 0.25, 1, (row == 7)[None], (lane == 127)[None], c1x, c1)
    for m in k2_all[:6]:
        m.wait_recv()
    level(k2[6:20], 12, 5, 2, 0.25 ** 2, 1, ((row & 3) == 3)[None], ((lane & 63) == 63)[None], c2x, c2)

    b_up.wait_recv()
    b_dn.wait_recv()
    for j in (0, 1, 2, 9, 10, 11):
        first_v(j)
    for j in (1, 2, 3, 8, 9, 10):
        second_v(j)
    for j in range(4):
        for c in range(3):
            both = fine_residue(x_buf, c, 2 * j + 2, 2 * j + 2) + fine_residue(x_buf, c, 2 * j + 3, 2 * j + 3)
            b1[c, 4 + j] = 0.125 * halve_fine(both, 4 + 3 * j + c)
    b1_up.start()
    b1_dn.start()

    rest = [share(b1[c, 4:8], c1x, c1) for c in range(3)]
    quarter = (row >= 4).astype(jnp.int32) * 2 + (lane >= 64).astype(jnp.int32)
    for j in range(4):
        parts = [halve_middle(r[2 * j] + r[2 * j + 1]) for r in rest]
        m2[3, j] = 0.125 * jnp.where(quarter == 0, parts[0], jnp.where(quarter == 1, parts[1], jnp.where(quarter == 2, parts[2], 0.0)))
    for m in m2_all:
        m.start()

    def halve_coarse(x):
        pairs = x.reshape(x.shape[0] // 2, 2, 8, 128)
        x = pairs[:, 0] + pairs[:, 1]
        x = x + gather(x, jnp.broadcast_to((row ^ 1)[None], x.shape), 1)
        return 0.125 * (x + gather(x, jnp.broadcast_to((lane ^ 1)[None], x.shape), 2))

    low = halve_coarse(widen(share(m2[3], c2x, c2), 1))
    odd_row, odd_lane = (row & 1) == 1, (lane & 1) == 1
    m3[7, 0] = jnp.where(odd_row, jnp.where(odd_lane, low[3], low[2]), jnp.where(odd_lane, low[1], low[0]))
    m3[7, 1] = low[4]
    for m in m3_all:
        m.start()
    x0_up.start()
    x0_dn.start()

    for m in k2_all[6:]:
        m.wait_recv()
    level(halve_coarse(k2[...]), 11, 5, 1, 0.25 ** 3, 2, ((row & 3) >= 2)[None], ((lane & 63) >= 62)[None], c3x, c3)

    for m in (b1_up, b1_dn, *m2_all, *m3_all):
        m.wait_recv()
    packed = m3[:, 0]

    def spots(index, count):
        return jnp.broadcast_to(index[None], (count, 8, 128))

    left, right = gather(packed, spots(lane & 126, 15), 2), gather(packed, spots(lane | 1, 15), 2)
    upper, lower = left[4:15] + right[3:14], left[2:13] + right[1:12]
    b3 = gather(upper, spots(row & 6, 11), 1) + gather(lower, spots(row | 1, 11), 1) + m3[0:11, 1]
    low = b3 * (c3[5] * (1.0 / bottom_roots[0]))
    for i in (1, 2, 3):
        inner = slice(i, 11 - i)
        low = low[1:-1] + apply(b3[inner], low, c3x, c3, 2, i, 11 - i) * (c3[5, inner] * (1.0 / bottom_roots[i]))
    b2 = jnp.stack([m2[3 + i // 2, 1] + m2[2 + i // 2, 3] if i % 2 == 0 else m2[3 + i // 2, 2] + m2[4 + i // 2, 0]
                    for i in range(-5, 7)])
    v = pre_smooth(b2, c2x, c2) + jnp.broadcast_to(low[:, None], (5, 2, 8, 128)).reshape(10, 8, 128)
    x = post_smooth(b2, v, c2x, c2)

    ups = []
    for c in range(3):
        spread = []
        for j in range(6):
            half = gather(x[j], 64 * (c % 2) + (lane >> 1), 1)
            spread.append(gather(half, 4 * (c // 2) + (row >> 1), 0))
        v = pre_smooth(b1[c], c1x, c1) + jnp.stack([spread[(i + 1) // 2] for i in range(10)])
        ups.append(post_smooth(b1[c], v, c1x, c1))

    x0_up.wait_recv()
    x0_dn.wait_recv()
    for j in range(6):
        for c in range(3):
            spread = []
            for h in range(2):
                part = gather(ups[c][j], 64 * h + (lane >> 1), 1)
                spread.append(jnp.concatenate([gather(part, row >> 1, 0), gather(part, 4 + (row >> 1), 0)], axis=0))
            spread = jnp.concatenate(spread, axis=1)
            for i in (2 * j, 2 * j + 1):
                s_buf[c, i] = x_buf[c, i] + spread
    for j in range(1, 11):
        for c in range(3):
            t_buf[c, j - 1] = s_buf[c, j] + fine_residue(s_buf, c, j, j) * db[j]
    for j in range(2, 10):
        for c in range(3):
            out_ref[c, j - 2] = t_buf[c, j - 1] + fine_residue(t_buf, c, j, j - 1) * da[j]
    for m in all_messages:
        m.wait_send()


def solution(mesh):
    wide, grp = mesh.shape["wide"], mesh.shape["grp"]

    def on_device(load, bins):
        def plane(*lead):
            return pltpu.VMEM((*lead, 16, 256), F32)

        def small(*lead):
            return pltpu.VMEM((*lead, 8, 128), F32)

        return pl.pallas_call(
            functools.partial(kernel, wide * grp, wide, grp),
            out_shape=pltpu.VMEM(load.shape, F32),
            in_specs=[pl.BlockSpec(memory_space=pl.ANY)] * 2,
            out_specs=pl.BlockSpec(memory_space=pltpu.VMEM),
            scratch_shapes=[
                pltpu.VMEM((14, 16, 256), jnp.int32), plane(3, 12), plane(14), plane(13),
                *[plane(12) for _ in range(7)],
                plane(3, 12), plane(3, 12), plane(3, 12), plane(3, 10),
                pltpu.VMEM((16, 2, 16, 128), F32),
                small(3, 12), small(14), small(13), small(8, 12),
                small(26), small(7, 4), small(13), small(8, 12),
                small(15, 2), small(12), small(8, 11),
                pltpu.SemaphoreType.DMA((REMOTE,)), pltpu.SemaphoreType.DMA((REMOTE,)), pltpu.SemaphoreType.DMA((2,)),
            ],
            compiler_params=pltpu.CompilerParams(
                collective_id=0, has_side_effects=True, vmem_limit_bytes=60 * 1024 * 1024),
        )(load, bins)

    return jax.shard_map(
        on_device,
        mesh=mesh,
        in_specs=(P(None, ("wide", "grp"), None, None), P(("wide", "grp"), None, None)),
        out_specs=P(None, ("wide", "grp"), None, None),
        check_vma=False,
    )
```

```python
import functools
import math

import jax
import jax.numpy as jnp
from jax import lax
from jax.experimental import pallas as pl
from jax.experimental.pallas import tpu as pltpu
from jax.sharding import PartitionSpec as P

MESH = pl.DeviceIdType.MESH
F32 = jnp.float32

mass_shift = 0.1
root_a = 1.15 + 0.85 * math.sqrt(0.5)
root_b = 1.15 - 0.85 * math.sqrt(0.5)
bottom_roots = (
    1.1 + 0.9 * math.cos(math.pi / 8),
    1.1 - 0.9 * math.cos(math.pi / 8),
    1.1 + 0.9 * math.cos(3 * math.pi / 8),
    1.1 - 0.9 * math.cos(3 * math.pi / 8),
)

REMOTE = 52
REACH_K, REACH_2, REACH_3 = 6, 3, 7
PAIRS = ((0, 0), (0, 1), (1, 0), (1, 1))


def inverse(x):
    guess = pltpu.reciprocal(x, approx=True)
    return guess * (2.0 - x * guess)


def harmonic(first, second, scale):
    return (2.0 * scale) * (first * second) * inverse(first + second)


def gather(x, index, axis):
    return jnp.take_along_axis(x, index, axis=axis, mode="promise_in_bounds")


def rolled(x, shift, axis):
    return pltpu.roll(x, shift % x.shape[axis], axis)


def planar_faces(k, scale, hop, row_end, lane_end):
    axis = k.ndim - 2
    rows_up = jnp.where(row_end, 0.0, harmonic(k, rolled(k, -hop, axis), scale))
    lanes_up = jnp.where(lane_end, 0.0, harmonic(k, rolled(k, -hop, axis + 1), scale))
    return rows_up, rolled(rows_up, hop, axis), lanes_up, rolled(lanes_up, hop, axis + 1)


def residue(b, v, before, after, c, hop):
    axis = v.ndim - 2
    first = (b - c[6] * v) + (c[0] * before + c[1] * after)
    second = c[2] * rolled(v, -hop, axis) + c[3] * rolled(v, hop, axis)
    third = c[4] * rolled(v, -hop, axis + 1) + c[5] * rolled(v, hop, axis + 1)
    return first + (second + third)


def kernel(n, wide, grp, load_ref, bins_ref, out_ref, load_raw, bins_raw, b0, k0, cx, cy, cz, dg, da, db,
           v0, x0, tmp, b1, k1, c1x, c1, k2, m2, c2x, c2, m3, c3x, c3, send, recv, local):
    p = lax.axis_index("wide") * grp + lax.axis_index("grp")
    numbers = iter(range(REMOTE))

    def place(distance):
        q = lax.rem(p + (distance + n), n)
        return {"wide": lax.div(q, grp), "grp": lax.rem(q, grp)}

    def there(distance):
        return p + distance < n if distance > 0 else p + distance >= 0

    class Message:
        def __init__(self, src, dst, distance):
            number = next(numbers)
            self.distance = distance
            self.copy = pltpu.make_async_remote_copy(
                src_ref=src, dst_ref=dst, send_sem=send.at[number], recv_sem=recv.at[number],
                device_id=place(distance), device_id_type=MESH)

        def start(self):
            pl.when(there(self.distance))(self.copy.start)

        def wait_send(self):
            pl.when(there(self.distance))(self.copy.wait_send)

        def wait_recv(self):
            pl.when(there(-self.distance))(self.copy.wait_recv)

    def both_ways(reach):
        return [d for step in range(1, reach + 1) for d in (step, -step)]

    k0_all = [Message(k0.at[8:11], k0.at[0:3], 1), Message(k0.at[3:6], k0.at[11:14], -1)]
    b0_all = [(Message(b0.at[c, 8:10], b0.at[c, 0:2], 1), Message(b0.at[c, 2:4], b0.at[c, 10:12], -1)) for c in range(3)]
    k1_all = [Message(k1.at[5:9], k1.at[1:5], 1), Message(k1.at[5:9], k1.at[9:13], -1),
              Message(k1.at[8], k1.at[0], 2), Message(k1.at[5], k1.at[13], -2)]
    b1_all = [(Message(b1.at[c, 4:8], b1.at[c, 0:4], 1), Message(b1.at[c, 4:8], b1.at[c, 8:12], -1)) for c in range(3)]
    x0_all = [Message(x0.at[:, 8], x0.at[:, 0], 1), Message(x0.at[:, 3], x0.at[:, 11], -1)]
    k2_all = [Message(k2.at[12:14], k2.at[12 - 2 * d:14 - 2 * d], d) for d in both_ways(REACH_K)]
    part = {3: slice(2, 4), -3: slice(0, 2)}
    m2_all = [Message(m2.at[3, part.get(d, slice(0, 4))], m2.at[3 - d, part.get(d, slice(0, 4))], d) for d in both_ways(REACH_2)]
    m3_all = [Message(m3.at[7], m3.at[7 - d], d) for d in both_ways(REACH_3)]
    all_messages = [*k0_all, *b0_all[0], *b0_all[1], *b0_all[2], *k1_all, *b1_all[0], *b1_all[1], *b1_all[2], *x0_all,
                    *k2_all, *m2_all, *m3_all]

    def start(messages):
        for m in messages:
            m.start()

    def receive(messages):
        for m in messages:
            m.wait_recv()

    @pl.when(jnp.logical_or(p < REACH_3, p >= n - REACH_3))
    def _():
        for halo in (slice(0, 3), slice(11, 14)):
            k0[halo] = jnp.ones((3, 4, 8, 128), F32)
        for halo in (slice(0, 2), slice(10, 12)):
            b0[:, halo] = jnp.zeros((3, 2, 4, 8, 128), F32)
        for j in (0, 11):
            x0[:, j] = jnp.zeros((3, 4, 8, 128), F32)
        k1[...] = jnp.ones_like(k1)
        b1[...] = jnp.zeros_like(b1)
        k2[...] = jnp.ones_like(k2)
        m2[...] = jnp.zeros_like(m2)
        m3[...] = jnp.zeros_like(m3)

    bins_in = [pltpu.make_async_copy(bins_ref.at[:, :, 128 * w:128 * w + 128], bins_raw.at[w], local.at[w]) for w in (0, 1)]
    load_in = [[pltpu.make_async_copy(load_ref.at[c, :, :, 128 * w:128 * w + 128], load_raw.at[w, c], local.at[2 + 2 * c + w])
                for w in (0, 1)] for c in range(3)]
    for copy in (*bins_in, *load_in[0], *load_in[1], *load_in[2]):
        copy.start()
    barrier = pltpu.get_barrier_semaphore()
    for d in both_ways(REACH_3):
        pl.when(there(d))(functools.partial(
            pl.semaphore_signal, barrier, inc=1, device_id=place(d), device_id_type=MESH))

    row = lax.broadcasted_iota(jnp.int32, (8, 128), 0)
    lane = lax.broadcasted_iota(jnp.int32, (8, 128), 1)

    def halve_middle(x):
        x = gather(x, (2 * lane) & 127, 1) + gather(x, (2 * lane + 1) & 127, 1)
        return gather(x, (2 * row) & 7, 0) + gather(x, (2 * row + 1) & 7, 0)

    def parted(halves):
        return [jnp.where(lane < 64, *(gather(halves[w][t], (2 * lane + h) & 127, 1) for w in (0, 1))) for t, h in PAIRS]

    def rows_of(ref, *index):
        return [[ref[(w, *index, pl.ds(t, 8, stride=2), slice(None))] for t in (0, 1)] for w in (0, 1)]

    def tiles(ref, *index):
        return [ref[(*index, q)] for q in range(4)]

    def put(ref, values, *index):
        for q, value in enumerate(values):
            ref[(*index, q)] = value

    for copy in bins_in:
        copy.wait()
    for j in range(8):
        halves = [[(1.0 - x.astype(F32) * 0.0625) ** 2 + 0.001 for x in half] for half in rows_of(bins_raw, j)]
        put(k0, parted(halves), 3 + j)
    for j in range(4):
        low, high = tiles(k0, 3 + 2 * j), tiles(k0, 4 + 2 * j)
        k1[5 + j] = 0.125 * (((low[0] + low[1]) + (low[2] + low[3])) + ((high[0] + high[1]) + (high[2] + high[3])))
    for j in range(2):
        k2[12 + j] = 0.125 * halve_middle(k1[5 + 2 * j] + k1[6 + 2 * j])
    for c in range(3):
        for copy in load_in[c]:
            copy.wait()
        for j in (0, 1, 6, 7, 2, 3, 4, 5):
            put(b0, parted(rows_of(load_raw, c, j)), c, 2 + j)

    pl.semaphore_wait(barrier, jnp.minimum(p, REACH_3) + jnp.minimum(n - 1 - p, REACH_3))
    start((*k0_all, *b0_all[0], *k1_all[:2], *k2_all[:6], *k1_all[2:], *b0_all[1], *b0_all[2], *k2_all[6:]))

    edges = (2 - 8 * p, 2 + 8 * (n - p))

    def x_face(f):
        inside = jnp.where(jnp.logical_or(f == edges[0], f == edges[1]), 0.0, 1.0)
        put(cx, [harmonic(first, second, 1.0) * inside for first, second in zip(tiles(k0, f), tiles(k0, f + 1))], f)

    def yz_faces(j):
        k = tiles(k0, j + 1)
        for ref, axis, last, (lows, highs) in ((cy, 0, row == 7, (k[0:2], k[2:4])), (cz, 1, lane == 127, (k[0::2], k[1::2]))):
            for i, (low, high) in enumerate(zip(lows, highs)):
                ref[j, i] = harmonic(low, high, 1.0)
                following = jnp.where(last, 0.0, harmonic(high, rolled(low, -1, axis), 1.0))
                ref[j, 2 + i] = following
                ref[j, 4 + i] = rolled(following, 1, axis)

    def diagonal(j):
        for q, (t, h) in enumerate(PAIRS):
            total = (mass_shift + (cx[j, q] + cx[j + 1, q])) + ((cy[j, h] + cy[j, 4 - 2 * t + h]) + (cz[j, t] + cz[j, 4 - 2 * h + t]))
            dg[j, q] = total
            inv = inverse(total)
            da[j, q] = inv * (1.0 / root_a)
            db[j, q] = inv * (1.0 / root_b)

    def fine_residue(b, v, before, after, j):
        result = []
        for q, (t, h) in enumerate(PAIRS):
            row_mate, lane_mate = v[2 * (1 - t) + h], v[2 * t + 1 - h]
            first = (b[q] - dg[j, q] * v[q]) + (cx[j, q] * before[q] + cx[j + 1, q] * after[q])
            second = cy[j, h] * row_mate + cy[j, 4 - 2 * t + h] * rolled(row_mate, 1 - 2 * t, 0)
            third = cz[j, t] * lane_mate + cz[j, 4 - 2 * h + t] * rolled(lane_mate, 1 - 2 * h, 1)
            result.append(first + (second + third))
        return result

    def first_v(c, j):
        v = [x * y for x, y in zip(tiles(b0, c, j), tiles(da, j))]
        put(v0, v, c, j)

    def second_v(c, j):
        v = tiles(v0, c, j)
        rest = fine_residue(tiles(b0, c, j), v, tiles(v0, c, j - 1), tiles(v0, c, j + 1), j)
        put(x0, [x + r * d for x, r, d in zip(v, rest, tiles(db, j))], c, j)

    def x_flux(c, f):
        flux = [cx[f, q] * (x0[c, f, q] - x0[c, f - 1, q]) for q in range(4)]
        return (flux[0] + flux[1]) + (flux[2] + flux[3])

    def block_sum(c, j):
        total, rows_up, lanes_up = [], [], []
        for i in (j, j + 1):
            b, x = tiles(b0, c, i), tiles(x0, c, i)
            total.append(((b[0] + b[1]) + (b[2] + b[3])) - mass_shift * ((x[0] + x[1]) + (x[2] + x[3])))
            for e in (0, 1):
                rows_up.append(cy[i, 2 + e] * (rolled(x[e], -1, 0) - x[2 + e]))
                lanes_up.append(cz[i, 2 + e] * (rolled(x[2 * e], -1, 1) - x[2 * e + 1]))
        rows_up = (rows_up[0] + rows_up[1]) + (rows_up[2] + rows_up[3])
        lanes_up = (lanes_up[0] + lanes_up[1]) + (lanes_up[2] + lanes_up[3])
        return (total[0] + total[1]) + ((rows_up - rolled(rows_up, 1, 0)) + (lanes_up - rolled(lanes_up, 1, 1)))

    for f in range(3, 10):
        x_face(f)
    for j in range(2, 10):
        yz_faces(j)
    for j in range(3, 9):
        diagonal(j)
    inner = []
    for c in range(3):
        for j in range(3, 9):
            first_v(c, j)
        for j in range(4, 8):
            second_v(c, j)
        middle = x_flux(c, 6)
        inner.append((block_sum(c, 4) + middle, block_sum(c, 6) - middle))

    receive(k0_all)
    for f in (0, 1, 2, 10, 11, 12):
        x_face(f)
    for j in (0, 1, 10, 11):
        yz_faces(j)
    for j in (0, 1, 2, 9, 10, 11):
        diagonal(j)

    def down(c):
        receive(b0_all[c])
        for j in (0, 1, 2, 9, 10, 11):
            first_v(c, j)
        for j in (1, 2, 3, 8, 9, 10):
            second_v(c, j)
        left, right = x_flux(c, 4), x_flux(c, 8)
        b1[c, 4] = 0.125 * (block_sum(c, 2) + (left - x_flux(c, 2)))
        b1[c, 5] = 0.125 * (inner[c][0] - left)
        b1[c, 6] = 0.125 * (inner[c][1] + right)
        b1[c, 7] = 0.125 * (block_sum(c, 8) + (x_flux(c, 10) - right))
        start(b1_all[c])

    down(0)

    def edge_mask(count, spot, each):
        face = lax.broadcasted_iota(jnp.int32, (count, 8, 128), 0)
        return jnp.logical_or(face == spot - each * p, face == spot + each * (n - p))

    def level(k, count, spot, each, scale, hop, row_end, lane_end, x_ref, ref):
        x_ref[...] = jnp.where(edge_mask(count + 1, spot, each), 0.0, harmonic(k[:-1], k[1:], scale))
        faces = planar_faces(k[1:-1], scale, hop, row_end, lane_end)
        for i, face in enumerate(faces):
            ref[i] = face
        total = (mass_shift + (x_ref[:-1] + x_ref[1:])) + ((faces[0] + faces[1]) + (faces[2] + faces[3]))
        ref[4] = total
        inv = inverse(total)
        ref[5] = inv
        ref[6] = inv * (1.0 / root_a)
        ref[7] = inv * (1.0 / root_b)

    def apply(b, v, x_ref, ref, hop, first, last):
        inner = slice(first, last)
        coeffs = (x_ref[inner], x_ref[first + 1:last + 1], ref[0, inner], ref[1, inner], ref[2, inner], ref[3, inner], ref[4, inner])
        return residue(b, v[1:-1], v[:-2], v[2:], coeffs, hop)

    def widen(x, by):
        none = jnp.zeros((by, 8, 128), F32)
        return jnp.concatenate([none, x, none], axis=0)

    def pre_smooth(b, x_ref, ref):
        v = b * ref[6]
        return v[1:-1] + apply(b[1:-1], v, x_ref, ref, 1, 1, 11) * ref[7, 1:11]

    def post_smooth(b, start, x_ref, ref):
        v = start[1:-1] + apply(b[2:10], start, x_ref, ref, 1, 2, 10) * ref[7, 2:10]
        return v[1:-1] + apply(b[3:9], v, x_ref, ref, 1, 3, 9) * ref[6, 3:9]

    def share(b, x_ref, ref):
        v = widen(b * ref[6, 4:8], 2)
        x = widen(v[1:-1] + apply(widen(b, 1), v, x_ref, ref, 1, 3, 9) * ref[7, 3:9], 2)
        return apply(widen(b, 2), x, x_ref, ref, 1, 2, 10)

    receive(k1_all)
    level(k1[...], 12, 4, 4, 0.25, 1, (row == 7)[None], (lane == 127)[None], c1x, c1)
    receive(k2_all[:6])
    level(k2[6:20], 12, 5, 2, 0.25 ** 2, 1, ((row & 3) == 3)[None], ((lane & 63) == 63)[None], c2x, c2)

    rest = [share(b1[0, 4:8], c1x, c1)]
    for c in (1, 2):
        down(c)
        rest.append(share(b1[c, 4:8], c1x, c1))
    quarter = (row >= 4).astype(jnp.int32) * 2 + (lane >= 64).astype(jnp.int32)
    for j in range(4):
        parts = [halve_middle(r[2 * j] + r[2 * j + 1]) for r in rest]
        m2[3, j] = 0.125 * jnp.where(quarter == 0, parts[0], jnp.where(quarter == 1, parts[1], jnp.where(quarter == 2, parts[2], 0.0)))
    start(m2_all)

    def halve_coarse(x):
        pairs = x.reshape(x.shape[0] // 2, 2, 8, 128)
        x = pairs[:, 0] + pairs[:, 1]
        x = x + gather(x, jnp.broadcast_to((row ^ 1)[None], x.shape), 1)
        return 0.125 * (x + gather(x, jnp.broadcast_to((lane ^ 1)[None], x.shape), 2))

    low = halve_coarse(widen(share(m2[3], c2x, c2), 1))
    odd_row, odd_lane = (row & 1) == 1, (lane & 1) == 1
    m3[7, 0] = jnp.where(odd_row, jnp.where(odd_lane, low[3], low[2]), jnp.where(odd_lane, low[1], low[0]))
    m3[7, 1] = low[4]
    start((*m3_all, *x0_all))

    receive(k2_all[6:])
    level(halve_coarse(k2[...]), 11, 5, 1, 0.25 ** 3, 2, ((row & 3) >= 2)[None], ((lane & 63) >= 62)[None], c3x, c3)

    smooth_1 = []
    for c in range(3):
        receive(b1_all[c])
        smooth_1.append(pre_smooth(b1[c], c1x, c1))
    receive(m2_all)
    b2 = jnp.stack([m2[3 + i // 2, 1] + m2[2 + i // 2, 3] if i % 2 == 0 else m2[3 + i // 2, 2] + m2[4 + i // 2, 0]
                    for i in range(-5, 7)])
    smooth_2 = pre_smooth(b2, c2x, c2)

    receive(m3_all)
    packed = m3[:, 0]

    def spots(index, count):
        return jnp.broadcast_to(index[None], (count, 8, 128))

    left, right = gather(packed, spots(lane & 126, 15), 2), gather(packed, spots(lane | 1, 15), 2)
    upper, lower = left[4:15] + right[3:14], left[2:13] + right[1:12]
    b3 = gather(upper, spots(row & 6, 11), 1) + gather(lower, spots(row | 1, 11), 1) + m3[0:11, 1]
    low = b3 * (c3[5] * (1.0 / bottom_roots[0]))
    for i in (1, 2, 3):
        inner = slice(i, 11 - i)
        low = low[1:-1] + apply(b3[inner], low, c3x, c3, 2, i, 11 - i) * (c3[5, inner] * (1.0 / bottom_roots[i]))
    v = smooth_2 + jnp.broadcast_to(low[:, None], (5, 2, 8, 128)).reshape(10, 8, 128)
    x = post_smooth(b2, v, c2x, c2)

    ups = []
    for c in range(3):
        spread = []
        for j in range(6):
            half = gather(x[j], 64 * (c % 2) + (lane >> 1), 1)
            spread.append(gather(half, 4 * (c // 2) + (row >> 1), 0))
        v = smooth_1[c] + jnp.stack([spread[(i + 1) // 2] for i in range(10)])
        ups.append(post_smooth(b1[c], v, c1x, c1))

    receive(x0_all)
    for c in range(3):
        field = [[x + ups[c][j // 2] for x in tiles(x0, c, j)] for j in range(12)]
        half_way = {}
        for j in range(1, 11):
            rest = fine_residue(tiles(b0, c, j), field[j], field[j - 1], field[j + 1], j)
            half_way[j] = [x + r * d for x, r, d in zip(field[j], rest, tiles(db, j))]
            if j >= 3:
                i = j - 1
                rest = fine_residue(tiles(b0, c, i), half_way[i], half_way[i - 1], half_way[i + 1], i)
                done = [x + r * d for x, r, d in zip(half_way[i], rest, tiles(da, i))]
                slot = 8 * c + i - 2
                for w in (0, 1):
                    for t in (0, 1):
                        spread = [gather(done[2 * t + h], 64 * w + (lane >> 1), 1) for h in (0, 1)]
                        tmp[slot, w, pl.ds(t, 8, stride=2), :] = jnp.where((lane & 1) == 0, spread[0], spread[1])
                    out_ref[c, i - 2, :, 128 * w:128 * w + 128] = tmp[slot, w]
    for m in all_messages:
        m.wait_send()


def solution(mesh):
    wide, grp = mesh.shape["wide"], mesh.shape["grp"]

    def on_device(load, bins):
        def plane(*lead):
            return pltpu.VMEM((*lead, 4, 8, 128), F32)

        def small(*lead):
            return pltpu.VMEM((*lead, 8, 128), F32)

        return pl.pallas_call(
            functools.partial(kernel, wide * grp, wide, grp),
            out_shape=pltpu.VMEM(load.shape, F32),
            in_specs=[pl.BlockSpec(memory_space=pl.ANY)] * 2,
            out_specs=pl.BlockSpec(memory_space=pltpu.VMEM),
            scratch_shapes=[
                pltpu.VMEM((2, 3, 8, 16, 128), F32), pltpu.VMEM((2, 8, 16, 128), jnp.int32),
                plane(3, 12), plane(14), plane(13), small(12, 6), small(12, 6), plane(12), plane(12), plane(12),
                plane(3, 12), plane(3, 12), pltpu.VMEM((24, 2, 16, 128), F32),
                small(3, 12), small(14), small(13), small(8, 12),
                small(26), small(7, 4), small(13), small(8, 12),
                small(15, 2), small(12), small(8, 11),
                pltpu.SemaphoreType.DMA((REMOTE,)), pltpu.SemaphoreType.DMA((REMOTE,)), pltpu.SemaphoreType.DMA((8,)),
            ],
            compiler_params=pltpu.CompilerParams(
                collective_id=0, has_side_effects=True, vmem_limit_bytes=60 * 1024 * 1024),
        )(load, bins)

    return jax.shard_map(
        on_device,
        mesh=mesh,
        in_specs=(P(None, ("wide", "grp"), None, None), P(("wide", "grp"), None, None)),
        out_specs=P(None, ("wide", "grp"), None, None),
        check_vma=False,
    )
```

```python
import functools
import itertools
import math

import jax
import jax.numpy as jnp
from jax import lax
from jax.experimental import pallas as pl
from jax.experimental.pallas import tpu as pltpu
from jax.sharding import PartitionSpec as P

MESH = pl.DeviceIdType.MESH
F32 = jnp.float32

mass_shift = 0.1
root_a = 1.15 + 0.85 * math.sqrt(0.5)
root_b = 1.15 - 0.85 * math.sqrt(0.5)
bottom_roots = (
    1.1 + 0.9 * math.cos(math.pi / 8),
    1.1 - 0.9 * math.cos(math.pi / 8),
    1.1 + 0.9 * math.cos(3 * math.pi / 8),
    1.1 - 0.9 * math.cos(3 * math.pi / 8),
)

REMOTE = 52
REACH_K, REACH_2, REACH_3 = 6, 3, 7
PAIRS = ((0, 0), (0, 1), (1, 0), (1, 1))


def inverse(x):
    guess = pltpu.reciprocal(x, approx=True)
    return guess * (2.0 - x * guess)


def harmonic(first, second, scale):
    return (2.0 * scale) * (first * second) * inverse(first + second)


def gather(x, index, axis):
    return jnp.take_along_axis(x, index, axis=axis, mode="promise_in_bounds")


def rolled(x, shift, axis):
    return pltpu.roll(x, shift % x.shape[axis], axis)


def planar_faces(k, scale, hop, row_end, lane_end):
    axis = k.ndim - 2
    rows_up = jnp.where(row_end, 0.0, harmonic(k, rolled(k, -hop, axis), scale))
    lanes_up = jnp.where(lane_end, 0.0, harmonic(k, rolled(k, -hop, axis + 1), scale))
    return rows_up, rolled(rows_up, hop, axis), lanes_up, rolled(lanes_up, hop, axis + 1)


def residue(b, v, before, after, c, hop):
    axis = v.ndim - 2
    first = (b - c[6] * v) + (c[0] * before + c[1] * after)
    second = c[2] * rolled(v, -hop, axis) + c[3] * rolled(v, hop, axis)
    third = c[4] * rolled(v, -hop, axis + 1) + c[5] * rolled(v, hop, axis + 1)
    return first + (second + third)


def kernel(n, wide, grp, load_ref, bins_ref, out_ref, load_raw, bins_raw, b0, k0, cx, cy, cz, dg, da, db,
           v0, x0, tmp, b1, k1, c1x, c1, k2, m2, c2x, c2, m3, c3x, c3, send, recv, local):
    p = lax.axis_index("wide") * grp + lax.axis_index("grp")
    numbers = iter(range(REMOTE))

    def place(distance):
        spot = lax.axis_index("grp") + distance
        if distance > 0:
            carry = jnp.where(spot >= grp, 1, 0)
        else:
            carry = jnp.where(spot < 0, -1, 0)
        return {"wide": lax.axis_index("wide") + carry, "grp": spot - carry * grp}

    def there(distance):
        return p + distance < n if distance > 0 else p + distance >= 0

    class Message:
        def __init__(self, src, dst, distance):
            number = next(numbers)
            self.distance = distance
            self.copy = pltpu.make_async_remote_copy(
                src_ref=src, dst_ref=dst, send_sem=send.at[number], recv_sem=recv.at[number],
                device_id=place(distance), device_id_type=MESH)

    def both_ways(reach):
        return [d for step in range(1, reach + 1) for d in (step, -step)]

    k0_all = [Message(k0.at[8:11], k0.at[0:3], 1), Message(k0.at[3:6], k0.at[11:14], -1)]
    b0_all = [(Message(b0.at[c, 8:10], b0.at[c, 0:2], 1), Message(b0.at[c, 2:4], b0.at[c, 10:12], -1)) for c in range(3)]
    k1_all = [Message(k1.at[5:9], k1.at[1:5], 1), Message(k1.at[5:9], k1.at[9:13], -1),
              Message(k1.at[8], k1.at[0], 2), Message(k1.at[5], k1.at[13], -2)]
    b1_all = [(Message(b1.at[c, 4:8], b1.at[c, 0:4], 1), Message(b1.at[c, 4:8], b1.at[c, 8:12], -1)) for c in range(3)]
    x0_all = [Message(x0.at[:, 8], x0.at[:, 0], 1), Message(x0.at[:, 3], x0.at[:, 11], -1)]
    k2_all = [Message(k2.at[12:14], k2.at[12 - 2 * d:14 - 2 * d], d) for d in both_ways(REACH_K)]
    part = {3: slice(2, 4), -3: slice(0, 2)}
    m2_all = [Message(m2.at[3, part.get(d, slice(0, 4))], m2.at[3 - d, part.get(d, slice(0, 4))], d) for d in both_ways(REACH_2)]
    m3_all = [Message(m3.at[7], m3.at[7 - d], d) for d in both_ways(REACH_3)]
    early = [*k0_all, *b0_all[0], *b0_all[1], *b0_all[2], *k1_all, *k2_all, *b1_all[0], *b1_all[1], *b1_all[2]]
    late = [*m3_all, *m2_all, *x0_all]

    def grouped(messages, sign, act):
        for distance, run in itertools.groupby(messages, lambda m: sign * m.distance):
            run = list(run)

            @pl.when(there(distance))
            def _():
                for m in run:
                    act(m.copy)

    def start(messages):
        grouped(messages, 1, lambda copy: copy.start())

    def finish(messages):
        grouped(sorted(messages, key=lambda m: m.distance), 1, lambda copy: copy.wait_send())

    def receive(messages):
        grouped(sorted(messages, key=lambda m: m.distance), -1, lambda copy: copy.wait_recv())

    @pl.when(jnp.logical_or(p < REACH_3, p >= n - REACH_3))
    def _():
        for halo in (slice(0, 3), slice(11, 14)):
            k0[halo] = jnp.ones((3, 4, 8, 128), F32)
        for halo in (slice(0, 2), slice(10, 12)):
            b0[:, halo] = jnp.zeros((3, 2, 4, 8, 128), F32)
        for j in (0, 11):
            x0[:, j] = jnp.zeros((3, 4, 8, 128), F32)
        k1[...] = jnp.ones_like(k1)
        b1[...] = jnp.zeros_like(b1)
        k2[...] = jnp.ones_like(k2)
        m2[...] = jnp.zeros_like(m2)
        m3[...] = jnp.zeros_like(m3)

    bins_in = [pltpu.make_async_copy(bins_ref.at[:, :, 128 * w:128 * w + 128], bins_raw.at[w], local.at[w]) for w in (0, 1)]
    load_in = [[pltpu.make_async_copy(load_ref.at[c, :, :, 128 * w:128 * w + 128], load_raw.at[w, c], local.at[2 + 2 * c + w])
                for w in (0, 1)] for c in range(3)]
    for copy in (*bins_in, *load_in[0], *load_in[1], *load_in[2]):
        copy.start()
    barrier = pltpu.get_barrier_semaphore()
    for d in both_ways(REACH_3):
        pl.when(there(d))(functools.partial(
            pl.semaphore_signal, barrier, inc=1, device_id=place(d), device_id_type=MESH))

    row = lax.broadcasted_iota(jnp.int32, (8, 128), 0)
    lane = lax.broadcasted_iota(jnp.int32, (8, 128), 1)

    def halve_middle(x):
        x = gather(x, (2 * lane) & 127, 1) + gather(x, (2 * lane + 1) & 127, 1)
        return gather(x, (2 * row) & 7, 0) + gather(x, (2 * row + 1) & 7, 0)

    def parted(halves):
        return [jnp.where(lane < 64, *(gather(halves[w][t], (2 * lane + h) & 127, 1) for w in (0, 1))) for t, h in PAIRS]

    def rows_of(ref, *index):
        return [[ref[(w, *index, pl.ds(t, 8, stride=2), slice(None))] for t in (0, 1)] for w in (0, 1)]

    def tiles(ref, *index):
        return [ref[(*index, q)] for q in range(4)]

    def put(ref, values, *index):
        for q, value in enumerate(values):
            ref[(*index, q)] = value

    for copy in bins_in:
        copy.wait()
    for j in range(8):
        halves = [[(1.0 - x.astype(F32) * 0.0625) ** 2 + 0.001 for x in half] for half in rows_of(bins_raw, j)]
        put(k0, parted(halves), 3 + j)
    for j in range(4):
        low, high = tiles(k0, 3 + 2 * j), tiles(k0, 4 + 2 * j)
        k1[5 + j] = 0.125 * (((low[0] + low[1]) + (low[2] + low[3])) + ((high[0] + high[1]) + (high[2] + high[3])))
    for j in range(2):
        k2[12 + j] = 0.125 * halve_middle(k1[5 + 2 * j] + k1[6 + 2 * j])
    for c in range(3):
        for copy in load_in[c]:
            copy.wait()
        for j in (0, 1, 6, 7, 2, 3, 4, 5):
            put(b0, parted(rows_of(load_raw, c, j)), c, 2 + j)

    pl.semaphore_wait(barrier, jnp.minimum(p, REACH_3) + jnp.minimum(n - 1 - p, REACH_3))
    start((k0_all[0], b0_all[0][0], k0_all[1], b0_all[0][1], *k1_all[:2], *k2_all[:6], *k1_all[2:], *b0_all[1], *b0_all[2], *k2_all[6:]))

    edges = (2 - 8 * p, 2 + 8 * (n - p))

    def x_face(f):
        inside = jnp.where(jnp.logical_or(f == edges[0], f == edges[1]), 0.0, 1.0)
        put(cx, [harmonic(first, second, 1.0) * inside for first, second in zip(tiles(k0, f), tiles(k0, f + 1))], f)

    def yz_faces(j):
        k = tiles(k0, j + 1)
        for ref, axis, last, (lows, highs) in ((cy, 0, row == 7, (k[0:2], k[2:4])), (cz, 1, lane == 127, (k[0::2], k[1::2]))):
            for i, (low, high) in enumerate(zip(lows, highs)):
                ref[j, i] = harmonic(low, high, 1.0)
                following = jnp.where(last, 0.0, harmonic(high, rolled(low, -1, axis), 1.0))
                ref[j, 2 + i] = following
                ref[j, 4 + i] = rolled(following, 1, axis)

    def diagonal(j):
        for q, (t, h) in enumerate(PAIRS):
            total = (mass_shift + (cx[j, q] + cx[j + 1, q])) + ((cy[j, h] + cy[j, 4 - 2 * t + h]) + (cz[j, t] + cz[j, 4 - 2 * h + t]))
            dg[j, q] = total
            inv = inverse(total)
            da[j, q] = inv * (1.0 / root_a)
            db[j, q] = inv * (1.0 / root_b)

    def fine_residue(b, v, before, after, j):
        result = []
        for q, (t, h) in enumerate(PAIRS):
            row_mate, lane_mate = v[2 * (1 - t) + h], v[2 * t + 1 - h]
            first = (b[q] - dg[j, q] * v[q]) + (cx[j, q] * before[q] + cx[j + 1, q] * after[q])
            second = cy[j, h] * row_mate + cy[j, 4 - 2 * t + h] * rolled(row_mate, 1 - 2 * t, 0)
            third = cz[j, t] * lane_mate + cz[j, 4 - 2 * h + t] * rolled(lane_mate, 1 - 2 * h, 1)
            result.append(first + (second + third))
        return result

    def first_v(c, j):
        v = [x * y for x, y in zip(tiles(b0, c, j), tiles(da, j))]
        put(v0, v, c, j)

    def second_v(c, j):
        v = tiles(v0, c, j)
        rest = fine_residue(tiles(b0, c, j), v, tiles(v0, c, j - 1), tiles(v0, c, j + 1), j)
        put(x0, [x + r * d for x, r, d in zip(v, rest, tiles(db, j))], c, j)

    def x_flux(c, f):
        flux = [cx[f, q] * (x0[c, f, q] - x0[c, f - 1, q]) for q in range(4)]
        return (flux[0] + flux[1]) + (flux[2] + flux[3])

    def block_sum(c, j):
        total, rows_up, lanes_up = [], [], []
        for i in (j, j + 1):
            b, x = tiles(b0, c, i), tiles(x0, c, i)
            total.append(((b[0] + b[1]) + (b[2] + b[3])) - mass_shift * ((x[0] + x[1]) + (x[2] + x[3])))
            for e in (0, 1):
                rows_up.append(cy[i, 2 + e] * (rolled(x[e], -1, 0) - x[2 + e]))
                lanes_up.append(cz[i, 2 + e] * (rolled(x[2 * e], -1, 1) - x[2 * e + 1]))
        rows_up = (rows_up[0] + rows_up[1]) + (rows_up[2] + rows_up[3])
        lanes_up = (lanes_up[0] + lanes_up[1]) + (lanes_up[2] + lanes_up[3])
        return (total[0] + total[1]) + ((rows_up - rolled(rows_up, 1, 0)) + (lanes_up - rolled(lanes_up, 1, 1)))

    for f in range(3, 10):
        x_face(f)
    for j in range(2, 10):
        yz_faces(j)
    for j in range(3, 9):
        diagonal(j)
    inner = []
    for c in range(3):
        for j in range(3, 9):
            first_v(c, j)
        for j in range(4, 8):
            second_v(c, j)
        middle = x_flux(c, 6)
        inner.append((block_sum(c, 4) + middle, block_sum(c, 6) - middle))

    receive(k0_all)
    for f in (0, 1, 2, 10, 11, 12):
        x_face(f)
    for j in (0, 1, 10, 11):
        yz_faces(j)
    for j in (0, 1, 2, 9, 10, 11):
        diagonal(j)

    def down(c):
        receive(b0_all[c])
        for j in (0, 1, 2, 9, 10, 11):
            first_v(c, j)
        for j in (1, 2, 3, 8, 9, 10):
            second_v(c, j)
        left, right = x_flux(c, 4), x_flux(c, 8)
        b1[c, 4] = 0.125 * (block_sum(c, 2) + (left - x_flux(c, 2)))
        b1[c, 5] = 0.125 * (inner[c][0] - left)
        b1[c, 6] = 0.125 * (inner[c][1] + right)
        b1[c, 7] = 0.125 * (block_sum(c, 8) + (x_flux(c, 10) - right))
        start(b1_all[c])

    down(0)

    def edge_mask(count, spot, each):
        face = lax.broadcasted_iota(jnp.int32, (count, 8, 128), 0)
        return jnp.logical_or(face == spot - each * p, face == spot + each * (n - p))

    def level(k, count, spot, each, scale, hop, row_end, lane_end, x_ref, ref):
        x_ref[...] = jnp.where(edge_mask(count + 1, spot, each), 0.0, harmonic(k[:-1], k[1:], scale))
        faces = planar_faces(k[1:-1], scale, hop, row_end, lane_end)
        for i, face in enumerate(faces):
            ref[i] = face
        total = (mass_shift + (x_ref[:-1] + x_ref[1:])) + ((faces[0] + faces[1]) + (faces[2] + faces[3]))
        ref[4] = total
        inv = inverse(total)
        ref[5] = inv
        ref[6] = inv * (1.0 / root_a)
        ref[7] = inv * (1.0 / root_b)

    def apply(b, v, x_ref, ref, hop, first, last):
        inner = slice(first, last)
        coeffs = (x_ref[inner], x_ref[first + 1:last + 1], ref[0, inner], ref[1, inner], ref[2, inner], ref[3, inner], ref[4, inner])
        return residue(b, v[1:-1], v[:-2], v[2:], coeffs, hop)

    def widen(x, by):
        none = jnp.zeros((by, 8, 128), F32)
        return jnp.concatenate([none, x, none], axis=0)

    def pre_smooth(b, x_ref, ref):
        v = b * ref[6]
        return v[1:-1] + apply(b[1:-1], v, x_ref, ref, 1, 1, 11) * ref[7, 1:11]

    def post_smooth(b, start, x_ref, ref):
        v = start[1:-1] + apply(b[2:10], start, x_ref, ref, 1, 2, 10) * ref[7, 2:10]
        return v[1:-1] + apply(b[3:9], v, x_ref, ref, 1, 3, 9) * ref[6, 3:9]

    def share(b, x_ref, ref):
        v = widen(b * ref[6, 4:8], 2)
        x = widen(v[1:-1] + apply(widen(b, 1), v, x_ref, ref, 1, 3, 9) * ref[7, 3:9], 2)
        return apply(widen(b, 2), x, x_ref, ref, 1, 2, 10)

    receive(k1_all)
    level(k1[...], 12, 4, 4, 0.25, 1, (row == 7)[None], (lane == 127)[None], c1x, c1)
    receive(k2_all[:6])
    level(k2[6:20], 12, 5, 2, 0.25 ** 2, 1, ((row & 3) == 3)[None], ((lane & 63) == 63)[None], c2x, c2)

    rest = [share(b1[0, 4:8], c1x, c1)]
    for c in (1, 2):
        down(c)
        rest.append(share(b1[c, 4:8], c1x, c1))
    quarter = (row >= 4).astype(jnp.int32) * 2 + (lane >= 64).astype(jnp.int32)
    for j in range(4):
        parts = [halve_middle(r[2 * j] + r[2 * j + 1]) for r in rest]
        m2[3, j] = 0.125 * jnp.where(quarter == 0, parts[0], jnp.where(quarter == 1, parts[1], jnp.where(quarter == 2, parts[2], 0.0)))

    def halve_coarse(x):
        pairs = x.reshape(x.shape[0] // 2, 2, 8, 128)
        x = pairs[:, 0] + pairs[:, 1]
        x = x + gather(x, jnp.broadcast_to((row ^ 1)[None], x.shape), 1)
        return 0.125 * (x + gather(x, jnp.broadcast_to((lane ^ 1)[None], x.shape), 2))

    low = halve_coarse(widen(share(m2[3], c2x, c2), 1))
    odd_row, odd_lane = (row & 1) == 1, (lane & 1) == 1
    m3[7, 0] = jnp.where(odd_row, jnp.where(odd_lane, low[3], low[2]), jnp.where(odd_lane, low[1], low[0]))
    m3[7, 1] = low[4]
    start((*m3_all, *m2_all, *x0_all))

    receive(k2_all[6:])
    level(halve_coarse(k2[...]), 11, 5, 1, 0.25 ** 3, 2, ((row & 3) >= 2)[None], ((lane & 63) >= 62)[None], c3x, c3)

    smooth_1 = []
    for c in range(3):
        receive(b1_all[c])
        smooth_1.append(pre_smooth(b1[c], c1x, c1))
    finish(early)
    receive(m3_all + m2_all)
    b2 = jnp.stack([m2[3 + i // 2, 1] + m2[2 + i // 2, 3] if i % 2 == 0 else m2[3 + i // 2, 2] + m2[4 + i // 2, 0]
                    for i in range(-5, 7)])
    smooth_2 = pre_smooth(b2, c2x, c2)

    packed = m3[:, 0]

    def spots(index, count):
        return jnp.broadcast_to(index[None], (count, 8, 128))

    left, right = gather(packed, spots(lane & 126, 15), 2), gather(packed, spots(lane | 1, 15), 2)
    upper, lower = left[4:15] + right[3:14], left[2:13] + right[1:12]
    b3 = gather(upper, spots(row & 6, 11), 1) + gather(lower, spots(row | 1, 11), 1) + m3[0:11, 1]
    low = b3 * (c3[5] * (1.0 / bottom_roots[0]))
    for i in (1, 2, 3):
        inner = slice(i, 11 - i)
        low = low[1:-1] + apply(b3[inner], low, c3x, c3, 2, i, 11 - i) * (c3[5, inner] * (1.0 / bottom_roots[i]))
    v = smooth_2 + jnp.broadcast_to(low[:, None], (5, 2, 8, 128)).reshape(10, 8, 128)
    x = post_smooth(b2, v, c2x, c2)

    ups = []
    for c in range(3):
        spread = []
        for j in range(6):
            half = gather(x[j], 64 * (c % 2) + (lane >> 1), 1)
            spread.append(gather(half, 4 * (c // 2) + (row >> 1), 0))
        v = smooth_1[c] + jnp.stack([spread[(i + 1) // 2] for i in range(10)])
        ups.append(post_smooth(b1[c], v, c1x, c1))

    receive(x0_all)
    for c in range(3):
        field = [[x + ups[c][j // 2] for x in tiles(x0, c, j)] for j in range(12)]
        half_way = {}
        for j in range(1, 11):
            rest = fine_residue(tiles(b0, c, j), field[j], field[j - 1], field[j + 1], j)
            half_way[j] = [x + r * d for x, r, d in zip(field[j], rest, tiles(db, j))]
            if j >= 3:
                i = j - 1
                rest = fine_residue(tiles(b0, c, i), half_way[i], half_way[i - 1], half_way[i + 1], i)
                done = [x + r * d for x, r, d in zip(half_way[i], rest, tiles(da, i))]
                slot = 8 * c + i - 2
                for w in (0, 1):
                    for t in (0, 1):
                        spread = [gather(done[2 * t + h], 64 * w + (lane >> 1), 1) for h in (0, 1)]
                        tmp[slot, w, pl.ds(t, 8, stride=2), :] = jnp.where((lane & 1) == 0, spread[0], spread[1])
                    out_ref[c, i - 2, :, 128 * w:128 * w + 128] = tmp[slot, w]
    finish(late)


def solution(mesh):
    wide, grp = mesh.shape["wide"], mesh.shape["grp"]

    def on_device(load, bins):
        def plane(*lead):
            return pltpu.VMEM((*lead, 4, 8, 128), F32)

        def small(*lead):
            return pltpu.VMEM((*lead, 8, 128), F32)

        return pl.pallas_call(
            functools.partial(kernel, wide * grp, wide, grp),
            out_shape=pltpu.VMEM(load.shape, F32),
            in_specs=[pl.BlockSpec(memory_space=pl.ANY)] * 2,
            out_specs=pl.BlockSpec(memory_space=pltpu.VMEM),
            scratch_shapes=[
                pltpu.VMEM((2, 3, 8, 16, 128), F32), pltpu.VMEM((2, 8, 16, 128), jnp.int32),
                plane(3, 12), plane(14), plane(13), small(12, 6), small(12, 6), plane(12), plane(12), plane(12),
                plane(3, 12), plane(3, 12), pltpu.VMEM((24, 2, 16, 128), F32),
                small(3, 12), small(14), small(13), small(8, 12),
                small(26), small(7, 4), small(13), small(8, 12),
                small(15, 2), small(12), small(8, 11),
                pltpu.SemaphoreType.DMA((REMOTE,)), pltpu.SemaphoreType.DMA((REMOTE,)), pltpu.SemaphoreType.DMA((8,)),
            ],
            compiler_params=pltpu.CompilerParams(
                collective_id=0, has_side_effects=True, vmem_limit_bytes=60 * 1024 * 1024),
        )(load, bins)

    return jax.shard_map(
        on_device,
        mesh=mesh,
        in_specs=(P(None, ("wide", "grp"), None, None), P(("wide", "grp"), None, None)),
        out_specs=P(None, ("wide", "grp"), None, None),
        check_vma=False,
    )
```

```python
import functools
import itertools
import math

import jax
import jax.numpy as jnp
from jax import lax
from jax.experimental import pallas as pl
from jax.experimental.pallas import tpu as pltpu
from jax.sharding import PartitionSpec as P

MESH = pl.DeviceIdType.MESH
F32 = jnp.float32

mass_shift = 0.1
root_a = 1.15 + 0.85 * math.sqrt(0.5)
root_b = 1.15 - 0.85 * math.sqrt(0.5)
bottom_roots = (
    1.1 + 0.9 * math.cos(math.pi / 8),
    1.1 - 0.9 * math.cos(math.pi / 8),
    1.1 + 0.9 * math.cos(3 * math.pi / 8),
    1.1 - 0.9 * math.cos(3 * math.pi / 8),
)

REMOTE = 52
REACH_K, REACH_2, REACH_3 = 6, 3, 7
PAIRS = ((0, 0), (0, 1), (1, 0), (1, 1))


def inverse(x):
    guess = pltpu.reciprocal(x, approx=True)
    return guess * (2.0 - x * guess)


def harmonic(first, second, scale):
    return (2.0 * scale) * (first * second) * inverse(first + second)


def gather(x, index, axis):
    return jnp.take_along_axis(x, index, axis=axis, mode="promise_in_bounds")


def rolled(x, shift, axis):
    return pltpu.roll(x, shift % x.shape[axis], axis)


def planar_faces(k, scale, hop, row_end, lane_end):
    axis = k.ndim - 2
    rows_up = jnp.where(row_end, 0.0, harmonic(k, rolled(k, -hop, axis), scale))
    lanes_up = jnp.where(lane_end, 0.0, harmonic(k, rolled(k, -hop, axis + 1), scale))
    return rows_up, rolled(rows_up, hop, axis), lanes_up, rolled(lanes_up, hop, axis + 1)


def residue(b, v, before, after, c, hop):
    axis = v.ndim - 2
    first = (b - c[6] * v) + (c[0] * before + c[1] * after)
    second = c[2] * rolled(v, -hop, axis) + c[3] * rolled(v, hop, axis)
    third = c[4] * rolled(v, -hop, axis + 1) + c[5] * rolled(v, hop, axis + 1)
    return first + (second + third)


def kernel(n, wide, grp, load_ref, bins_ref, out_ref, load_raw, bins_raw, b0, k0, cx, cy, cz, dg, da, db,
           v0, x0, tmp, b1, k1, c1x, c1, k2, m2, c2x, c2, m3, c3x, c3, send, recv, local):
    p = lax.axis_index("wide") * grp + lax.axis_index("grp")
    numbers = iter(range(REMOTE))

    def place(distance):
        spot = lax.axis_index("grp") + distance
        if distance > 0:
            carry = jnp.where(spot >= grp, 1, 0)
        else:
            carry = jnp.where(spot < 0, -1, 0)
        return {"wide": lax.axis_index("wide") + carry, "grp": spot - carry * grp}

    def there(distance):
        return p + distance < n if distance > 0 else p + distance >= 0

    class Message:
        def __init__(self, src, dst, distance):
            number = next(numbers)
            self.distance = distance
            self.copy = pltpu.make_async_remote_copy(
                src_ref=src, dst_ref=dst, send_sem=send.at[number], recv_sem=recv.at[number],
                device_id=place(distance), device_id_type=MESH)

    def both_ways(reach):
        return [d for step in range(1, reach + 1) for d in (step, -step)]

    k0_all = [Message(k0.at[8:11], k0.at[0:3], 1), Message(k0.at[3:6], k0.at[11:14], -1)]
    b0_all = [(Message(b0.at[c, 8:10], b0.at[c, 0:2], 1), Message(b0.at[c, 2:4], b0.at[c, 10:12], -1)) for c in range(3)]
    k1_all = [Message(k1.at[5:9], k1.at[1:5], 1), Message(k1.at[5:9], k1.at[9:13], -1),
              Message(k1.at[8], k1.at[0], 2), Message(k1.at[5], k1.at[13], -2)]
    b1_all = [(Message(b1.at[c, 4:8], b1.at[c, 0:4], 1), Message(b1.at[c, 4:8], b1.at[c, 8:12], -1)) for c in range(3)]
    x0_all = [Message(x0.at[:, 8], x0.at[:, 0], 1), Message(x0.at[:, 3], x0.at[:, 11], -1)]
    k2_all = [Message(k2.at[6], k2.at[6 - d], d) for d in both_ways(REACH_K)]
    part = {3: slice(2, 4), -3: slice(0, 2)}
    m2_all = [Message(m2.at[3, part.get(d, slice(0, 4))], m2.at[3 - d, part.get(d, slice(0, 4))], d) for d in both_ways(REACH_2)]
    m3_all = [Message(m3.at[7], m3.at[7 - d], d) for d in both_ways(REACH_3)]
    early = [*k0_all, *b0_all[0], *b0_all[1], *b0_all[2], *k1_all, *k2_all, *b1_all[0], *b1_all[1], *b1_all[2]]
    late = [*m3_all, *m2_all, *x0_all]

    def grouped(messages, sign, act):
        for distance, run in itertools.groupby(messages, lambda m: sign * m.distance):
            run = list(run)

            @pl.when(there(distance))
            def _():
                for m in run:
                    act(m.copy)

    def start(messages):
        grouped(messages, 1, lambda copy: copy.start())

    def finish(messages):
        grouped(sorted(messages, key=lambda m: m.distance), 1, lambda copy: copy.wait_send())

    def receive(messages):
        grouped(sorted(messages, key=lambda m: m.distance), -1, lambda copy: copy.wait_recv())

    @pl.when(jnp.logical_or(p < REACH_3, p >= n - REACH_3))
    def _():
        for halo in (slice(0, 3), slice(11, 14)):
            k0[halo] = jnp.ones((3, 4, 8, 128), F32)
        for halo in (slice(0, 2), slice(10, 12)):
            b0[:, halo] = jnp.zeros((3, 2, 4, 8, 128), F32)
        for j in (0, 11):
            x0[:, j] = jnp.zeros((3, 4, 8, 128), F32)
        k1[...] = jnp.ones_like(k1)
        b1[...] = jnp.zeros_like(b1)
        k2[...] = jnp.ones_like(k2)
        m2[...] = jnp.zeros_like(m2)
        m3[...] = jnp.zeros_like(m3)

    bins_in = [pltpu.make_async_copy(bins_ref.at[:, :, 128 * w:128 * w + 128], bins_raw.at[w], local.at[w]) for w in (0, 1)]
    load_in = [[pltpu.make_async_copy(load_ref.at[c, :, :, 128 * w:128 * w + 128], load_raw.at[w, c], local.at[2 + 2 * c + w])
                for w in (0, 1)] for c in range(3)]
    for copy in (*bins_in, *load_in[0], *load_in[1], *load_in[2]):
        copy.start()
    barrier = pltpu.get_barrier_semaphore()
    for d in both_ways(REACH_3):
        pl.when(there(d))(functools.partial(
            pl.semaphore_signal, barrier, inc=1, device_id=place(d), device_id_type=MESH))

    row = lax.broadcasted_iota(jnp.int32, (8, 128), 0)
    lane = lax.broadcasted_iota(jnp.int32, (8, 128), 1)

    def halve_middle(x):
        x = gather(x, (2 * lane) & 127, 1) + gather(x, (2 * lane + 1) & 127, 1)
        return gather(x, (2 * row) & 7, 0) + gather(x, (2 * row + 1) & 7, 0)

    def parted(halves):
        return [jnp.where(lane < 64, *(gather(halves[w][t], (2 * lane + h) & 127, 1) for w in (0, 1))) for t, h in PAIRS]

    def rows_of(ref, *index):
        return [[ref[(w, *index, pl.ds(t, 8, stride=2), slice(None))] for t in (0, 1)] for w in (0, 1)]

    def tiles(ref, *index):
        return [ref[(*index, q)] for q in range(4)]

    def put(ref, values, *index):
        for q, value in enumerate(values):
            ref[(*index, q)] = value

    for copy in bins_in:
        copy.wait()
    for j in range(8):
        halves = [[(1.0 - x.astype(F32) * 0.0625) ** 2 + 0.001 for x in half] for half in rows_of(bins_raw, j)]
        put(k0, parted(halves), 3 + j)
    for j in range(4):
        low, high = tiles(k0, 3 + 2 * j), tiles(k0, 4 + 2 * j)
        k1[5 + j] = 0.125 * (((low[0] + low[1]) + (low[2] + low[3])) + ((high[0] + high[1]) + (high[2] + high[3])))
    k2[6] = 0.125 * jnp.where(row < 4, halve_middle(k1[5] + k1[6]), halve_middle(k1[7] + k1[8]))
    for c in range(3):
        for copy in load_in[c]:
            copy.wait()
        for j in (0, 1, 6, 7, 2, 3, 4, 5):
            put(b0, parted(rows_of(load_raw, c, j)), c, 2 + j)

    pl.semaphore_wait(barrier, jnp.minimum(p, REACH_3) + jnp.minimum(n - 1 - p, REACH_3))
    start((k0_all[0], b0_all[0][0], k0_all[1], b0_all[0][1], *k1_all[:2], *k2_all[:6], *k1_all[2:], *b0_all[1], *b0_all[2], *k2_all[6:]))

    edges = (2 - 8 * p, 2 + 8 * (n - p))

    def x_face(f):
        inside = jnp.where(jnp.logical_or(f == edges[0], f == edges[1]), 0.0, 1.0)
        put(cx, [harmonic(first, second, 1.0) * inside for first, second in zip(tiles(k0, f), tiles(k0, f + 1))], f)

    def yz_faces(j):
        k = tiles(k0, j + 1)
        for ref, axis, last, (lows, highs) in ((cy, 0, row == 7, (k[0:2], k[2:4])), (cz, 1, lane == 127, (k[0::2], k[1::2]))):
            for i, (low, high) in enumerate(zip(lows, highs)):
                ref[j, i] = harmonic(low, high, 1.0)
                following = jnp.where(last, 0.0, harmonic(high, rolled(low, -1, axis), 1.0))
                ref[j, 2 + i] = following
                ref[j, 4 + i] = rolled(following, 1, axis)

    def diagonal(j):
        for q, (t, h) in enumerate(PAIRS):
            total = (mass_shift + (cx[j, q] + cx[j + 1, q])) + ((cy[j, h] + cy[j, 4 - 2 * t + h]) + (cz[j, t] + cz[j, 4 - 2 * h + t]))
            dg[j, q] = total
            inv = inverse(total)
            da[j, q] = inv * (1.0 / root_a)
            db[j, q] = inv * (1.0 / root_b)

    def fine_residue(b, v, before, after, j):
        result = []
        for q, (t, h) in enumerate(PAIRS):
            row_mate, lane_mate = v[2 * (1 - t) + h], v[2 * t + 1 - h]
            first = (b[q] - dg[j, q] * v[q]) + (cx[j, q] * before[q] + cx[j + 1, q] * after[q])
            second = cy[j, h] * row_mate + cy[j, 4 - 2 * t + h] * rolled(row_mate, 1 - 2 * t, 0)
            third = cz[j, t] * lane_mate + cz[j, 4 - 2 * h + t] * rolled(lane_mate, 1 - 2 * h, 1)
            result.append(first + (second + third))
        return result

    def first_v(c, j):
        v = [x * y for x, y in zip(tiles(b0, c, j), tiles(da, j))]
        put(v0, v, c, j)

    def second_v(c, j):
        v = tiles(v0, c, j)
        rest = fine_residue(tiles(b0, c, j), v, tiles(v0, c, j - 1), tiles(v0, c, j + 1), j)
        put(x0, [x + r * d for x, r, d in zip(v, rest, tiles(db, j))], c, j)

    def x_flux(c, f):
        flux = [cx[f, q] * (x0[c, f, q] - x0[c, f - 1, q]) for q in range(4)]
        return (flux[0] + flux[1]) + (flux[2] + flux[3])

    def block_sum(c, j):
        total, rows_up, lanes_up = [], [], []
        for i in (j, j + 1):
            b, x = tiles(b0, c, i), tiles(x0, c, i)
            total.append(((b[0] + b[1]) + (b[2] + b[3])) - mass_shift * ((x[0] + x[1]) + (x[2] + x[3])))
            for e in (0, 1):
                rows_up.append(cy[i, 2 + e] * (rolled(x[e], -1, 0) - x[2 + e]))
                lanes_up.append(cz[i, 2 + e] * (rolled(x[2 * e], -1, 1) - x[2 * e + 1]))
        rows_up = (rows_up[0] + rows_up[1]) + (rows_up[2] + rows_up[3])
        lanes_up = (lanes_up[0] + lanes_up[1]) + (lanes_up[2] + lanes_up[3])
        return (total[0] + total[1]) + ((rows_up - rolled(rows_up, 1, 0)) + (lanes_up - rolled(lanes_up, 1, 1)))

    for f in range(3, 10):
        x_face(f)
    for j in range(2, 10):
        yz_faces(j)
    for j in range(3, 9):
        diagonal(j)
    inner = []
    for c in range(3):
        for j in range(3, 9):
            first_v(c, j)
        for j in range(4, 8):
            second_v(c, j)
        middle = x_flux(c, 6)
        inner.append((block_sum(c, 4) + middle, block_sum(c, 6) - middle))

    receive(k0_all)
    for f in (0, 1, 2, 10, 11, 12):
        x_face(f)
    for j in (0, 1, 10, 11):
        yz_faces(j)
    for j in (0, 1, 2, 9, 10, 11):
        diagonal(j)

    def down(c):
        receive(b0_all[c])
        for j in (0, 1, 2, 9, 10, 11):
            first_v(c, j)
        for j in (1, 2, 3, 8, 9, 10):
            second_v(c, j)
        left, right = x_flux(c, 4), x_flux(c, 8)
        b1[c, 4] = 0.125 * (block_sum(c, 2) + (left - x_flux(c, 2)))
        b1[c, 5] = 0.125 * (inner[c][0] - left)
        b1[c, 6] = 0.125 * (inner[c][1] + right)
        b1[c, 7] = 0.125 * (block_sum(c, 8) + (x_flux(c, 10) - right))
        start(b1_all[c])

    down(0)

    def edge_mask(count, spot, each):
        face = lax.broadcasted_iota(jnp.int32, (count, 8, 128), 0)
        return jnp.logical_or(face == spot - each * p, face == spot + each * (n - p))

    def level(k, count, spot, each, scale, hop, row_end, lane_end, x_ref, ref):
        x_ref[...] = jnp.where(edge_mask(count + 1, spot, each), 0.0, harmonic(k[:-1], k[1:], scale))
        faces = planar_faces(k[1:-1], scale, hop, row_end, lane_end)
        for i, face in enumerate(faces):
            ref[i] = face
        total = (mass_shift + (x_ref[:-1] + x_ref[1:])) + ((faces[0] + faces[1]) + (faces[2] + faces[3]))
        ref[4] = total
        inv = inverse(total)
        ref[5] = inv
        ref[6] = inv * (1.0 / root_a)
        ref[7] = inv * (1.0 / root_b)

    def apply(b, v, x_ref, ref, hop, first, last):
        inner = slice(first, last)
        coeffs = (x_ref[inner], x_ref[first + 1:last + 1], ref[0, inner], ref[1, inner], ref[2, inner], ref[3, inner], ref[4, inner])
        return residue(b, v[1:-1], v[:-2], v[2:], coeffs, hop)

    def widen(x, by):
        none = jnp.zeros((by, 8, 128), F32)
        return jnp.concatenate([none, x, none], axis=0)

    def pre_smooth(b, x_ref, ref):
        v = b * ref[6]
        return v[1:-1] + apply(b[1:-1], v, x_ref, ref, 1, 1, 11) * ref[7, 1:11]

    def post_smooth(b, start, x_ref, ref):
        v = start[1:-1] + apply(b[2:10], start, x_ref, ref, 1, 2, 10) * ref[7, 2:10]
        return v[1:-1] + apply(b[3:9], v, x_ref, ref, 1, 3, 9) * ref[6, 3:9]

    def share(b, x_ref, ref):
        v = widen(b * ref[6, 4:8], 2)
        x = widen(v[1:-1] + apply(widen(b, 1), v, x_ref, ref, 1, 3, 9) * ref[7, 3:9], 2)
        return apply(widen(b, 2), x, x_ref, ref, 1, 2, 10)

    receive(k1_all)
    level(k1[...], 12, 4, 4, 0.25, 1, (row == 7)[None], (lane == 127)[None], c1x, c1)
    receive(k2_all[:6])
    near = k2[3:10]
    turned = rolled(near, 4, 1)
    near = jnp.stack([jnp.where(row < 4, near, turned), jnp.where(row < 4, turned, near)], axis=1).reshape(14, 8, 128)
    level(near, 12, 5, 2, 0.25 ** 2, 1, ((row & 3) == 3)[None], ((lane & 63) == 63)[None], c2x, c2)

    rest = [share(b1[0, 4:8], c1x, c1)]
    for c in (1, 2):
        down(c)
        rest.append(share(b1[c, 4:8], c1x, c1))
    quarter = (row >= 4).astype(jnp.int32) * 2 + (lane >= 64).astype(jnp.int32)
    for j in range(4):
        parts = [halve_middle(r[2 * j] + r[2 * j + 1]) for r in rest]
        m2[3, j] = 0.125 * jnp.where(quarter == 0, parts[0], jnp.where(quarter == 1, parts[1], jnp.where(quarter == 2, parts[2], 0.0)))

    start(m2_all)

    def halve_coarse(first, second):
        x = first + second
        x = x + gather(x, jnp.broadcast_to((row ^ 1)[None], x.shape), 1)
        return 0.125 * (x + gather(x, jnp.broadcast_to((lane ^ 1)[None], x.shape), 2))

    rest = widen(share(m2[3], c2x, c2), 1).reshape(5, 2, 8, 128)
    low = halve_coarse(rest[:, 0], rest[:, 1])
    odd_row, odd_lane = (row & 1) == 1, (lane & 1) == 1
    four = jnp.where(odd_row, jnp.where(odd_lane, low[3], low[2]), jnp.where(odd_lane, low[1], low[0]))
    last = rolled(low[4], 64, 1)
    last = jnp.where(odd_row, last, rolled(jnp.where(odd_lane, low[4], last), 4, 0))
    m3[7] = jnp.where(quarter == 3, last, four)
    start((*m3_all, *x0_all))

    receive(k2_all[6:])
    level(halve_coarse(k2[...], rolled(k2[...], 4, 1)), 11, 5, 1, 0.25 ** 3, 2, ((row & 3) >= 2)[None], ((lane & 63) >= 62)[None], c3x, c3)

    smooth_1 = []
    for c in range(3):
        receive(b1_all[c])
        smooth_1.append(pre_smooth(b1[c], c1x, c1))
    receive(m2_all)
    b2 = jnp.stack([m2[3 + i // 2, 1] + m2[2 + i // 2, 3] if i % 2 == 0 else m2[3 + i // 2, 2] + m2[4 + i // 2, 0]
                    for i in range(-5, 7)])
    smooth_2 = pre_smooth(b2, c2x, c2)

    receive(m3_all)
    packed = m3[...]

    def spots(index, count):
        return jnp.broadcast_to(index[None], (count, 8, 128))

    left, right = gather(packed, spots(lane & 126, 15), 2), gather(packed, spots(lane | 1, 15), 2)
    upper, lower = left[4:15] + right[3:14], left[2:13] + right[1:12]
    last = gather(packed[0:11], spots(jnp.where(lane < 64, 64 + (lane & 126), lane | 1), 11), 2)
    last = gather(last, spots(jnp.where(row < 4, 4 + (row & 6), row | 1), 11), 1)
    b3 = gather(upper, spots(row & 6, 11), 1) + gather(lower, spots(row | 1, 11), 1) + last
    low = b3 * (c3[5] * (1.0 / bottom_roots[0]))
    for i in (1, 2, 3):
        inner = slice(i, 11 - i)
        low = low[1:-1] + apply(b3[inner], low, c3x, c3, 2, i, 11 - i) * (c3[5, inner] * (1.0 / bottom_roots[i]))
    v = smooth_2 + jnp.broadcast_to(low[:, None], (5, 2, 8, 128)).reshape(10, 8, 128)
    x = post_smooth(b2, v, c2x, c2)

    ups = []
    for c in range(3):
        spread = []
        for j in range(6):
            half = gather(x[j], 64 * (c % 2) + (lane >> 1), 1)
            spread.append(gather(half, 4 * (c // 2) + (row >> 1), 0))
        v = smooth_1[c] + jnp.stack([spread[(i + 1) // 2] for i in range(10)])
        ups.append(post_smooth(b1[c], v, c1x, c1))

    receive(x0_all)
    for c in range(3):
        field = [[x + ups[c][j // 2] for x in tiles(x0, c, j)] for j in range(12)]
        half_way = {}
        for j in range(1, 11):
            rest = fine_residue(tiles(b0, c, j), field[j], field[j - 1], field[j + 1], j)
            half_way[j] = [x + r * d for x, r, d in zip(field[j], rest, tiles(db, j))]
            if j >= 3:
                i = j - 1
                rest = fine_residue(tiles(b0, c, i), half_way[i], half_way[i - 1], half_way[i + 1], i)
                done = [x + r * d for x, r, d in zip(half_way[i], rest, tiles(da, i))]
                slot = 8 * c + i - 2
                for w in (0, 1):
                    for t in (0, 1):
                        spread = [gather(done[2 * t + h], 64 * w + (lane >> 1), 1) for h in (0, 1)]
                        tmp[slot, w, pl.ds(t, 8, stride=2), :] = jnp.where((lane & 1) == 0, spread[0], spread[1])
                    out_ref[c, i - 2, :, 128 * w:128 * w + 128] = tmp[slot, w]
    finish(early + late)


def solution(mesh):
    wide, grp = mesh.shape["wide"], mesh.shape["grp"]

    def on_device(load, bins):
        def plane(*lead):
            return pltpu.VMEM((*lead, 4, 8, 128), F32)

        def small(*lead):
            return pltpu.VMEM((*lead, 8, 128), F32)

        return pl.pallas_call(
            functools.partial(kernel, wide * grp, wide, grp),
            out_shape=pltpu.VMEM(load.shape, F32),
            in_specs=[pl.BlockSpec(memory_space=pl.ANY)] * 2,
            out_specs=pl.BlockSpec(memory_space=pltpu.VMEM),
            scratch_shapes=[
                pltpu.VMEM((2, 3, 8, 16, 128), F32), pltpu.VMEM((2, 8, 16, 128), jnp.int32),
                plane(3, 12), plane(14), plane(13), small(12, 6), small(12, 6), plane(12), plane(12), plane(12),
                plane(3, 12), plane(3, 12), pltpu.VMEM((24, 2, 16, 128), F32),
                small(3, 12), small(14), small(13), small(8, 12),
                small(13), small(7, 4), small(13), small(8, 12),
                small(15), small(12), small(8, 11),
                pltpu.SemaphoreType.DMA((REMOTE,)), pltpu.SemaphoreType.DMA((REMOTE,)), pltpu.SemaphoreType.DMA((8,)),
            ],
            compiler_params=pltpu.CompilerParams(
                collective_id=0, has_side_effects=True, vmem_limit_bytes=60 * 1024 * 1024),
        )(load, bins)

    return jax.shard_map(
        on_device,
        mesh=mesh,
        in_specs=(P(None, ("wide", "grp"), None, None), P(("wide", "grp"), None, None)),
        out_specs=P(None, ("wide", "grp"), None, None),
        check_vma=False,
    )
```

```python
import functools
import itertools
import math

import jax
import jax.numpy as jnp
from jax import lax
from jax.experimental import pallas as pl
from jax.experimental.pallas import tpu as pltpu
from jax.sharding import PartitionSpec as P

MESH = pl.DeviceIdType.MESH
F32 = jnp.float32

mass_shift = 0.1
root_a = 1.15 + 0.85 * math.sqrt(0.5)
root_b = 1.15 - 0.85 * math.sqrt(0.5)
bottom_roots = (
    1.1 + 0.9 * math.cos(math.pi / 8),
    1.1 - 0.9 * math.cos(math.pi / 8),
    1.1 + 0.9 * math.cos(3 * math.pi / 8),
    1.1 - 0.9 * math.cos(3 * math.pi / 8),
)

REMOTE = 54
REACH_K, REACH_2, REACH_3 = 6, 3, 7
PAIRS = ((0, 0), (0, 1), (1, 0), (1, 1))


def inverse(x):
    guess = pltpu.reciprocal(x, approx=True)
    return guess * (2.0 - x * guess)


def harmonic(first, second, scale):
    return (2.0 * scale) * (first * second) * inverse(first + second)


def gather(x, index, axis):
    return jnp.take_along_axis(x, index, axis=axis, mode="promise_in_bounds")


def rolled(x, shift, axis):
    return pltpu.roll(x, shift % x.shape[axis], axis)


def planar_faces(k, scale, hop, row_end, lane_end):
    axis = k.ndim - 2
    rows_up = jnp.where(row_end, 0.0, harmonic(k, rolled(k, -hop, axis), scale))
    lanes_up = jnp.where(lane_end, 0.0, harmonic(k, rolled(k, -hop, axis + 1), scale))
    return rows_up, rolled(rows_up, hop, axis), lanes_up, rolled(lanes_up, hop, axis + 1)


def residue(b, v, before, after, c, hop):
    axis = v.ndim - 2
    first = (b - c[6] * v) + (c[0] * before + c[1] * after)
    second = c[2] * rolled(v, -hop, axis) + c[3] * rolled(v, hop, axis)
    third = c[4] * rolled(v, -hop, axis + 1) + c[5] * rolled(v, hop, axis + 1)
    return first + (second + third)


def kernel(n, wide, grp, load_ref, bins_ref, out_ref, load_raw, bins_raw, b0, k0, cx, cy, cz, dg, da, db,
           v0, x0, tmp, b1, k1, c1x, c1, k2, m2, c2x, c2, m3, c3x, c3, send, recv, local):
    p = lax.axis_index("wide") * grp + lax.axis_index("grp")
    numbers = iter(range(REMOTE))

    def place(distance):
        spot = lax.axis_index("grp") + distance
        if distance > 0:
            carry = jnp.where(spot >= grp, 1, 0)
        else:
            carry = jnp.where(spot < 0, -1, 0)
        return {"wide": lax.axis_index("wide") + carry, "grp": spot - carry * grp}

    def there(distance):
        return p + distance < n if distance > 0 else p + distance >= 0

    class Message:
        def __init__(self, src, dst, distance):
            number = next(numbers)
            self.distance = distance
            self.copy = pltpu.make_async_remote_copy(
                src_ref=src, dst_ref=dst, send_sem=send.at[number], recv_sem=recv.at[number],
                device_id=place(distance), device_id_type=MESH)

    def both_ways(reach):
        return [d for step in range(1, reach + 1) for d in (step, -step)]

    k0_all = [Message(k0.at[9:12], k0.at[1:4], 1), Message(k0.at[4:7], k0.at[12:15], -1)]
    b0_all = [(Message(b0.at[c, 9:11], b0.at[c, 1:3], 1), Message(b0.at[c, 3:5], b0.at[c, 11:13], -1)) for c in range(3)]
    k1_all = [Message(k1.at[5:9], k1.at[1:5], 1), Message(k1.at[5:9], k1.at[9:13], -1),
              Message(k1.at[8], k1.at[0], 2), Message(k1.at[5], k1.at[13], -2)]
    b1_all = [(Message(b1.at[c, 4:8], b1.at[c, 0:4], 1), Message(b1.at[c, 4:8], b1.at[c, 8:12], -1)) for c in range(3)]
    outer_all = [Message(k0.at[8], k0.at[0], 1), Message(k0.at[7], k0.at[15], -1),
                 Message(b0.at[:, 8], b0.at[:, 0], 1), Message(b0.at[:, 5], b0.at[:, 13], -1)]
    k2_all = [Message(k2.at[6], k2.at[6 - d], d) for d in both_ways(REACH_K)]
    part = {3: slice(2, 4), -3: slice(0, 2)}
    m2_all = [Message(m2.at[3, part.get(d, slice(0, 4))], m2.at[3 - d, part.get(d, slice(0, 4))], d) for d in both_ways(REACH_2)]
    m3_all = [Message(m3.at[7], m3.at[7 - d], d) for d in both_ways(REACH_3)]
    early = [*outer_all, *k0_all, *b0_all[0], *b0_all[1], *b0_all[2], *k1_all, *k2_all, *b1_all[0], *b1_all[1], *b1_all[2]]
    late = [*m3_all, *m2_all]

    def grouped(messages, sign, act):
        for distance, run in itertools.groupby(messages, lambda m: sign * m.distance):
            run = list(run)

            @pl.when(there(distance))
            def _():
                for m in run:
                    act(m.copy)

    def start(messages):
        grouped(messages, 1, lambda copy: copy.start())

    def finish(messages):
        grouped(sorted(messages, key=lambda m: m.distance), 1, lambda copy: copy.wait_send())

    def receive(messages):
        grouped(sorted(messages, key=lambda m: m.distance), -1, lambda copy: copy.wait_recv())

    @pl.when(jnp.logical_or(p < REACH_3, p >= n - REACH_3))
    def _():
        for halo in (slice(0, 4), slice(12, 16)):
            k0[halo] = jnp.ones((4, 4, 8, 128), F32)
        for halo in (slice(0, 3), slice(11, 14)):
            b0[:, halo] = jnp.zeros((3, 3, 4, 8, 128), F32)
        k1[...] = jnp.ones_like(k1)
        b1[...] = jnp.zeros_like(b1)
        k2[...] = jnp.ones_like(k2)
        m2[...] = jnp.zeros_like(m2)
        m3[...] = jnp.zeros_like(m3)

    bins_in = [pltpu.make_async_copy(bins_ref.at[:, :, 128 * w:128 * w + 128], bins_raw.at[w], local.at[w]) for w in (0, 1)]
    load_in = [[pltpu.make_async_copy(load_ref.at[c, :, :, 128 * w:128 * w + 128], load_raw.at[w, c], local.at[2 + 2 * c + w])
                for w in (0, 1)] for c in range(3)]
    for copy in (*bins_in, *load_in[0], *load_in[1], *load_in[2]):
        copy.start()
    barrier = pltpu.get_barrier_semaphore()
    for d in both_ways(REACH_3):
        pl.when(there(d))(functools.partial(
            pl.semaphore_signal, barrier, inc=1, device_id=place(d), device_id_type=MESH))

    row = lax.broadcasted_iota(jnp.int32, (8, 128), 0)
    lane = lax.broadcasted_iota(jnp.int32, (8, 128), 1)

    def halve_middle(x):
        x = gather(x, (2 * lane) & 127, 1) + gather(x, (2 * lane + 1) & 127, 1)
        return gather(x, (2 * row) & 7, 0) + gather(x, (2 * row + 1) & 7, 0)

    def parted(halves):
        return [jnp.where(lane < 64, *(gather(halves[w][t], (2 * lane + h) & 127, 1) for w in (0, 1))) for t, h in PAIRS]

    def rows_of(ref, *index):
        return [[ref[(w, *index, pl.ds(t, 8, stride=2), slice(None))] for t in (0, 1)] for w in (0, 1)]

    def tiles(ref, *index):
        return [ref[(*index, q)] for q in range(4)]

    def put(ref, values, *index):
        for q, value in enumerate(values):
            ref[(*index, q)] = value

    for copy in bins_in:
        copy.wait()
    for j in range(8):
        halves = [[(1.0 - x.astype(F32) * 0.0625) ** 2 + 0.001 for x in half] for half in rows_of(bins_raw, j)]
        put(k0, parted(halves), 4 + j)
    for j in range(4):
        low, high = tiles(k0, 4 + 2 * j), tiles(k0, 5 + 2 * j)
        k1[5 + j] = 0.125 * (((low[0] + low[1]) + (low[2] + low[3])) + ((high[0] + high[1]) + (high[2] + high[3])))
    k2[6] = 0.125 * jnp.where(row < 4, halve_middle(k1[5] + k1[6]), halve_middle(k1[7] + k1[8]))
    for c in range(3):
        for copy in load_in[c]:
            copy.wait()
        for j in (0, 1, 6, 7, 2, 3, 4, 5):
            put(b0, parted(rows_of(load_raw, c, j)), c, 3 + j)

    pl.semaphore_wait(barrier, jnp.minimum(p, REACH_3) + jnp.minimum(n - 1 - p, REACH_3))
    start((k0_all[0], b0_all[0][0], k0_all[1], b0_all[0][1], *k1_all[:2], *k2_all[:6], *k1_all[2:], *b0_all[1], *b0_all[2], *outer_all, *k2_all[6:]))

    edges = (3 - 8 * p, 3 + 8 * (n - p))

    def x_face(f):
        inside = jnp.where(jnp.logical_or(f == edges[0], f == edges[1]), 0.0, 1.0)
        put(cx, [harmonic(first, second, 1.0) * inside for first, second in zip(tiles(k0, f), tiles(k0, f + 1))], f)

    def yz_faces(j):
        k = tiles(k0, j + 1)
        for ref, axis, last, (lows, highs) in ((cy, 0, row == 7, (k[0:2], k[2:4])), (cz, 1, lane == 127, (k[0::2], k[1::2]))):
            for i, (low, high) in enumerate(zip(lows, highs)):
                ref[j, i] = harmonic(low, high, 1.0)
                following = jnp.where(last, 0.0, harmonic(high, rolled(low, -1, axis), 1.0))
                ref[j, 2 + i] = following
                ref[j, 4 + i] = rolled(following, 1, axis)

    def diagonal(j):
        for q, (t, h) in enumerate(PAIRS):
            total = (mass_shift + (cx[j, q] + cx[j + 1, q])) + ((cy[j, h] + cy[j, 4 - 2 * t + h]) + (cz[j, t] + cz[j, 4 - 2 * h + t]))
            dg[j, q] = total
            inv = inverse(total)
            da[j, q] = inv * (1.0 / root_a)
            db[j, q] = inv * (1.0 / root_b)

    def fine_residue(b, v, before, after, j):
        result = []
        for q, (t, h) in enumerate(PAIRS):
            row_mate, lane_mate = v[2 * (1 - t) + h], v[2 * t + 1 - h]
            first = (b[q] - dg[j, q] * v[q]) + (cx[j, q] * before[q] + cx[j + 1, q] * after[q])
            second = cy[j, h] * row_mate + cy[j, 4 - 2 * t + h] * rolled(row_mate, 1 - 2 * t, 0)
            third = cz[j, t] * lane_mate + cz[j, 4 - 2 * h + t] * rolled(lane_mate, 1 - 2 * h, 1)
            result.append(first + (second + third))
        return result

    def first_v(c, j):
        v = [x * y for x, y in zip(tiles(b0, c, j), tiles(da, j))]
        put(v0, v, c, j)

    def second_v(c, j):
        v = tiles(v0, c, j)
        rest = fine_residue(tiles(b0, c, j), v, tiles(v0, c, j - 1), tiles(v0, c, j + 1), j)
        put(x0, [x + r * d for x, r, d in zip(v, rest, tiles(db, j))], c, j)

    def x_flux(c, f):
        flux = [cx[f, q] * (x0[c, f, q] - x0[c, f - 1, q]) for q in range(4)]
        return (flux[0] + flux[1]) + (flux[2] + flux[3])

    def block_sum(c, j):
        total, rows_up, lanes_up = [], [], []
        for i in (j, j + 1):
            b, x = tiles(b0, c, i), tiles(x0, c, i)
            total.append(((b[0] + b[1]) + (b[2] + b[3])) - mass_shift * ((x[0] + x[1]) + (x[2] + x[3])))
            for e in (0, 1):
                rows_up.append(cy[i, 2 + e] * (rolled(x[e], -1, 0) - x[2 + e]))
                lanes_up.append(cz[i, 2 + e] * (rolled(x[2 * e], -1, 1) - x[2 * e + 1]))
        rows_up = (rows_up[0] + rows_up[1]) + (rows_up[2] + rows_up[3])
        lanes_up = (lanes_up[0] + lanes_up[1]) + (lanes_up[2] + lanes_up[3])
        return (total[0] + total[1]) + ((rows_up - rolled(rows_up, 1, 0)) + (lanes_up - rolled(lanes_up, 1, 1)))

    for f in range(4, 11):
        x_face(f)
    for j in range(3, 11):
        yz_faces(j)
    for j in range(4, 10):
        diagonal(j)
    inner = []
    for c in range(3):
        for j in range(4, 10):
            first_v(c, j)
        for j in range(5, 9):
            second_v(c, j)
        middle = x_flux(c, 7)
        inner.append((block_sum(c, 5) + middle, block_sum(c, 7) - middle))

    receive(k0_all)
    for f in (1, 2, 3, 11, 12, 13):
        x_face(f)
    for j in (1, 2, 11, 12):
        yz_faces(j)
    for j in (1, 2, 3, 10, 11, 12):
        diagonal(j)

    def down(c):
        receive(b0_all[c])
        for j in (1, 2, 3, 10, 11, 12):
            first_v(c, j)
        for j in (2, 3, 4, 9, 10, 11):
            second_v(c, j)
        left, right = x_flux(c, 5), x_flux(c, 9)
        b1[c, 4] = 0.125 * (block_sum(c, 3) + (left - x_flux(c, 3)))
        b1[c, 5] = 0.125 * (inner[c][0] - left)
        b1[c, 6] = 0.125 * (inner[c][1] + right)
        b1[c, 7] = 0.125 * (block_sum(c, 9) + (x_flux(c, 11) - right))
        start(b1_all[c])

    down(0)

    def edge_mask(count, spot, each):
        face = lax.broadcasted_iota(jnp.int32, (count, 8, 128), 0)
        return jnp.logical_or(face == spot - each * p, face == spot + each * (n - p))

    def level(k, count, spot, each, scale, hop, row_end, lane_end, x_ref, ref):
        x_ref[...] = jnp.where(edge_mask(count + 1, spot, each), 0.0, harmonic(k[:-1], k[1:], scale))
        faces = planar_faces(k[1:-1], scale, hop, row_end, lane_end)
        for i, face in enumerate(faces):
            ref[i] = face
        total = (mass_shift + (x_ref[:-1] + x_ref[1:])) + ((faces[0] + faces[1]) + (faces[2] + faces[3]))
        ref[4] = total
        inv = inverse(total)
        ref[5] = inv
        ref[6] = inv * (1.0 / root_a)
        ref[7] = inv * (1.0 / root_b)

    def apply(b, v, x_ref, ref, hop, first, last):
        inner = slice(first, last)
        coeffs = (x_ref[inner], x_ref[first + 1:last + 1], ref[0, inner], ref[1, inner], ref[2, inner], ref[3, inner], ref[4, inner])
        return residue(b, v[1:-1], v[:-2], v[2:], coeffs, hop)

    def widen(x, by):
        none = jnp.zeros((by, 8, 128), F32)
        return jnp.concatenate([none, x, none], axis=0)

    def pre_smooth(b, x_ref, ref):
        v = b * ref[6]
        return v[1:-1] + apply(b[1:-1], v, x_ref, ref, 1, 1, 11) * ref[7, 1:11]

    def post_smooth(b, start, x_ref, ref):
        v = start[1:-1] + apply(b[2:10], start, x_ref, ref, 1, 2, 10) * ref[7, 2:10]
        return v[1:-1] + apply(b[3:9], v, x_ref, ref, 1, 3, 9) * ref[6, 3:9]

    def share(b, x_ref, ref):
        v = widen(b * ref[6, 4:8], 2)
        x = widen(v[1:-1] + apply(widen(b, 1), v, x_ref, ref, 1, 3, 9) * ref[7, 3:9], 2)
        return apply(widen(b, 2), x, x_ref, ref, 1, 2, 10)

    receive(k1_all)
    level(k1[...], 12, 4, 4, 0.25, 1, (row == 7)[None], (lane == 127)[None], c1x, c1)
    receive(k2_all[:6])
    near = k2[3:10]
    turned = rolled(near, 4, 1)
    near = jnp.stack([jnp.where(row < 4, near, turned), jnp.where(row < 4, turned, near)], axis=1).reshape(14, 8, 128)
    level(near, 12, 5, 2, 0.25 ** 2, 1, ((row & 3) == 3)[None], ((lane & 63) == 63)[None], c2x, c2)

    rest = [share(b1[0, 4:8], c1x, c1)]
    for c in (1, 2):
        down(c)
        rest.append(share(b1[c, 4:8], c1x, c1))
    quarter = (row >= 4).astype(jnp.int32) * 2 + (lane >= 64).astype(jnp.int32)
    for j in range(4):
        parts = [halve_middle(r[2 * j] + r[2 * j + 1]) for r in rest]
        m2[3, j] = 0.125 * jnp.where(quarter == 0, parts[0], jnp.where(quarter == 1, parts[1], jnp.where(quarter == 2, parts[2], 0.0)))

    start(m2_all)

    def halve_coarse(first, second):
        x = first + second
        x = x + gather(x, jnp.broadcast_to((row ^ 1)[None], x.shape), 1)
        return 0.125 * (x + gather(x, jnp.broadcast_to((lane ^ 1)[None], x.shape), 2))

    rest = widen(share(m2[3], c2x, c2), 1).reshape(5, 2, 8, 128)
    low = halve_coarse(rest[:, 0], rest[:, 1])
    odd_row, odd_lane = (row & 1) == 1, (lane & 1) == 1
    four = jnp.where(odd_row, jnp.where(odd_lane, low[3], low[2]), jnp.where(odd_lane, low[1], low[0]))
    last = rolled(low[4], 64, 1)
    last = jnp.where(odd_row, last, rolled(jnp.where(odd_lane, low[4], last), 4, 0))
    m3[7] = jnp.where(quarter == 3, last, four)
    start(m3_all)

    receive(k2_all[6:])
    level(halve_coarse(k2[...], rolled(k2[...], 4, 1)), 11, 5, 1, 0.25 ** 3, 2, ((row & 3) >= 2)[None], ((lane & 63) >= 62)[None], c3x, c3)

    receive(outer_all)
    for f in (0, 14):
        x_face(f)
    for j in (0, 13):
        yz_faces(j)
        diagonal(j)
    for c in range(3):
        for j in (0, 13):
            first_v(c, j)
        for j in (1, 12):
            second_v(c, j)

    smooth_1 = []
    for c in range(3):
        receive(b1_all[c])
        smooth_1.append(pre_smooth(b1[c], c1x, c1))
    receive(m2_all)
    b2 = jnp.stack([m2[3 + i // 2, 1] + m2[2 + i // 2, 3] if i % 2 == 0 else m2[3 + i // 2, 2] + m2[4 + i // 2, 0]
                    for i in range(-5, 7)])
    smooth_2 = pre_smooth(b2, c2x, c2)

    receive(m3_all)
    packed = m3[...]

    def spots(index, count):
        return jnp.broadcast_to(index[None], (count, 8, 128))

    left, right = gather(packed, spots(lane & 126, 15), 2), gather(packed, spots(lane | 1, 15), 2)
    upper, lower = left[4:15] + right[3:14], left[2:13] + right[1:12]
    last = gather(packed[0:11], spots(jnp.where(lane < 64, 64 + (lane & 126), lane | 1), 11), 2)
    last = gather(last, spots(jnp.where(row < 4, 4 + (row & 6), row | 1), 11), 1)
    b3 = gather(upper, spots(row & 6, 11), 1) + gather(lower, spots(row | 1, 11), 1) + last
    low = b3 * (c3[5] * (1.0 / bottom_roots[0]))
    for i in (1, 2, 3):
        inner = slice(i, 11 - i)
        low = low[1:-1] + apply(b3[inner], low, c3x, c3, 2, i, 11 - i) * (c3[5, inner] * (1.0 / bottom_roots[i]))
    v = smooth_2 + jnp.broadcast_to(low[:, None], (5, 2, 8, 128)).reshape(10, 8, 128)
    x = post_smooth(b2, v, c2x, c2)

    ups = []
    for c in range(3):
        spread = []
        for j in range(6):
            half = gather(x[j], 64 * (c % 2) + (lane >> 1), 1)
            spread.append(gather(half, 4 * (c // 2) + (row >> 1), 0))
        v = smooth_1[c] + jnp.stack([spread[(i + 1) // 2] for i in range(10)])
        ups.append(post_smooth(b1[c], v, c1x, c1))

    for c in range(3):
        field = [None] + [[x + ups[c][(j - 1) // 2] for x in tiles(x0, c, j)] for j in range(1, 13)]
        half_way = {}
        for j in range(2, 12):
            rest = fine_residue(tiles(b0, c, j), field[j], field[j - 1], field[j + 1], j)
            half_way[j] = [x + r * d for x, r, d in zip(field[j], rest, tiles(db, j))]
            if j >= 4:
                i = j - 1
                rest = fine_residue(tiles(b0, c, i), half_way[i], half_way[i - 1], half_way[i + 1], i)
                done = [x + r * d for x, r, d in zip(half_way[i], rest, tiles(da, i))]
                slot = 8 * c + i - 3
                for w in (0, 1):
                    for t in (0, 1):
                        spread = [gather(done[2 * t + h], 64 * w + (lane >> 1), 1) for h in (0, 1)]
                        tmp[slot, w, pl.ds(t, 8, stride=2), :] = jnp.where((lane & 1) == 0, spread[0], spread[1])
                    out_ref[c, i - 3, :, 128 * w:128 * w + 128] = tmp[slot, w]
    finish(early + late)


def solution(mesh):
    wide, grp = mesh.shape["wide"], mesh.shape["grp"]

    def on_device(load, bins):
        def plane(*lead):
            return pltpu.VMEM((*lead, 4, 8, 128), F32)

        def small(*lead):
            return pltpu.VMEM((*lead, 8, 128), F32)

        return pl.pallas_call(
            functools.partial(kernel, wide * grp, wide, grp),
            out_shape=pltpu.VMEM(load.shape, F32),
            in_specs=[pl.BlockSpec(memory_space=pl.ANY)] * 2,
            out_specs=pl.BlockSpec(memory_space=pltpu.VMEM),
            scratch_shapes=[
                pltpu.VMEM((2, 3, 8, 16, 128), F32), pltpu.VMEM((2, 8, 16, 128), jnp.int32),
                plane(3, 14), plane(16), plane(15), small(14, 6), small(14, 6), plane(14), plane(14), plane(14),
                plane(3, 14), plane(3, 14), pltpu.VMEM((24, 2, 16, 128), F32),
                small(3, 12), small(14), small(13), small(8, 12),
                small(13), small(7, 4), small(13), small(8, 12),
                small(15), small(12), small(8, 11),
                pltpu.SemaphoreType.DMA((REMOTE,)), pltpu.SemaphoreType.DMA((REMOTE,)), pltpu.SemaphoreType.DMA((8,)),
            ],
            compiler_params=pltpu.CompilerParams(
                collective_id=0, has_side_effects=True, vmem_limit_bytes=60 * 1024 * 1024),
        )(load, bins)

    return jax.shard_map(
        on_device,
        mesh=mesh,
        in_specs=(P(None, ("wide", "grp"), None, None), P(("wide", "grp"), None, None)),
        out_specs=P(None, ("wide", "grp"), None, None),
        check_vma=False,
    )
```

```python
import functools
import itertools
import math

import jax
import jax.numpy as jnp
from jax import lax
from jax.experimental import pallas as pl
from jax.experimental.pallas import tpu as pltpu
from jax.sharding import PartitionSpec as P

MESH = pl.DeviceIdType.MESH
F32 = jnp.float32

mass_shift = 0.1
root_a = 1.15 + 0.85 * math.sqrt(0.5)
root_b = 1.15 - 0.85 * math.sqrt(0.5)
bottom_roots = (
    1.1 + 0.9 * math.cos(math.pi / 8),
    1.1 - 0.9 * math.cos(math.pi / 8),
    1.1 + 0.9 * math.cos(3 * math.pi / 8),
    1.1 - 0.9 * math.cos(3 * math.pi / 8),
)

REMOTE = 54
REACH_K, REACH_2, REACH_3 = 6, 3, 7
PAIRS = ((0, 0), (0, 1), (1, 0), (1, 1))


def inverse(x):
    guess = pltpu.reciprocal(x, approx=True)
    return guess * (2.0 - x * guess)


def harmonic(first, second, scale):
    return (2.0 * scale) * (first * second) * inverse(first + second)


def gather(x, index, axis):
    return jnp.take_along_axis(x, index, axis=axis, mode="promise_in_bounds")


def rolled(x, shift, axis):
    return pltpu.roll(x, shift % x.shape[axis], axis)


def planar_faces(k, scale, hop, row_end, lane_end):
    axis = k.ndim - 2
    rows_up = jnp.where(row_end, 0.0, harmonic(k, rolled(k, -hop, axis), scale))
    lanes_up = jnp.where(lane_end, 0.0, harmonic(k, rolled(k, -hop, axis + 1), scale))
    return rows_up, rolled(rows_up, hop, axis), lanes_up, rolled(lanes_up, hop, axis + 1)


def residue(b, v, before, after, c, hop):
    axis = v.ndim - 2
    first = (b - c[6] * v) + (c[0] * before + c[1] * after)
    second = c[2] * rolled(v, -hop, axis) + c[3] * rolled(v, hop, axis)
    third = c[4] * rolled(v, -hop, axis + 1) + c[5] * rolled(v, hop, axis + 1)
    return first + (second + third)


def kernel(n, wide, grp, load_ref, bins_ref, out_ref, load_raw, bins_raw, b0, k0, cx, cy, cz, dg, da, db,
           v0, x0, tmp, b1, k1, c1x, c1, k2, m2, c2x, c2, m3, c3x, c3, send, recv, local):
    p = lax.axis_index("wide") * grp + lax.axis_index("grp")
    numbers = iter(range(REMOTE))

    def place(distance):
        spot = lax.axis_index("grp") + distance
        if distance > 0:
            carry = jnp.where(spot >= grp, 1, 0)
        else:
            carry = jnp.where(spot < 0, -1, 0)
        return {"wide": lax.axis_index("wide") + carry, "grp": spot - carry * grp}

    def there(distance):
        return p + distance < n if distance > 0 else p + distance >= 0

    class Message:
        def __init__(self, src, dst, distance):
            number = next(numbers)
            self.distance = distance
            self.copy = pltpu.make_async_remote_copy(
                src_ref=src, dst_ref=dst, send_sem=send.at[number], recv_sem=recv.at[number],
                device_id=place(distance), device_id_type=MESH)

    def both_ways(reach):
        return [d for step in range(1, reach + 1) for d in (step, -step)]

    k0_all = [Message(k0.at[9:12], k0.at[1:4], 1), Message(k0.at[4:7], k0.at[12:15], -1)]
    b0_all = [(Message(b0.at[c, 9:11], b0.at[c, 1:3], 1), Message(b0.at[c, 3:5], b0.at[c, 11:13], -1)) for c in range(3)]
    k1_all = [Message(k1.at[5:9], k1.at[1:5], 1), Message(k1.at[5:9], k1.at[9:13], -1),
              Message(k1.at[8], k1.at[0], 2), Message(k1.at[5], k1.at[13], -2)]
    b1_all = [(Message(b1.at[c, 4:8], b1.at[c, 0:4], 1), Message(b1.at[c, 4:8], b1.at[c, 8:12], -1)) for c in range(3)]
    outer_all = [Message(k0.at[8], k0.at[0], 1), Message(k0.at[7], k0.at[15], -1),
                 Message(b0.at[:, 8], b0.at[:, 0], 1), Message(b0.at[:, 5], b0.at[:, 13], -1)]
    k2_all = [Message(k2.at[6], k2.at[6 - d], d) for d in both_ways(REACH_K)]
    part = {3: slice(2, 4), -3: slice(0, 2)}
    m2_all = [Message(m2.at[3, part.get(d, slice(0, 4))], m2.at[3 - d, part.get(d, slice(0, 4))], d) for d in both_ways(REACH_2)]
    m3_all = [Message(m3.at[7], m3.at[7 - d], d) for d in both_ways(REACH_3)]
    early = [*outer_all, *k0_all, *b0_all[0], *b0_all[1], *b0_all[2], *k1_all, *k2_all, *b1_all[0], *b1_all[1], *b1_all[2]]
    late = [*m3_all, *m2_all]

    def grouped(messages, sign, act):
        for distance, run in itertools.groupby(messages, lambda m: sign * m.distance):
            run = list(run)

            @pl.when(there(distance))
            def _():
                for m in run:
                    act(m.copy)

    def start(messages):
        grouped(messages, 1, lambda copy: copy.start())

    def finish(messages):
        grouped(sorted(messages, key=lambda m: m.distance), 1, lambda copy: copy.wait_send())

    def receive(messages):
        grouped(sorted(messages, key=lambda m: m.distance), -1, lambda copy: copy.wait_recv())

    @pl.when(jnp.logical_or(p < REACH_3, p >= n - REACH_3))
    def _():
        for halo in (slice(0, 4), slice(12, 16)):
            k0[halo] = jnp.ones((4, 4, 8, 128), F32)
        for halo in (slice(0, 3), slice(11, 14)):
            b0[:, halo] = jnp.zeros((3, 3, 4, 8, 128), F32)
        k1[...] = jnp.ones_like(k1)
        b1[...] = jnp.zeros_like(b1)
        k2[...] = jnp.ones_like(k2)
        m2[...] = jnp.zeros_like(m2)
        m3[...] = jnp.zeros_like(m3)

    barrier = pltpu.get_barrier_semaphore()
    for d in both_ways(REACH_3):
        pl.when(there(d))(functools.partial(
            pl.semaphore_signal, barrier, inc=1, device_id=place(d), device_id_type=MESH))

    bins_in = [pltpu.make_async_copy(bins_ref.at[:, :, 128 * w:128 * w + 128], bins_raw.at[w], local.at[w]) for w in (0, 1)]
    load_in = [[pltpu.make_async_copy(load_ref.at[c, :, :, 128 * w:128 * w + 128], load_raw.at[w, c], local.at[2 + 2 * c + w])
                for w in (0, 1)] for c in range(3)]
    for copy in (*bins_in, *load_in[0], *load_in[1], *load_in[2]):
        copy.start()
    row = lax.broadcasted_iota(jnp.int32, (8, 128), 0)
    lane = lax.broadcasted_iota(jnp.int32, (8, 128), 1)

    def halve_middle(x):
        x = gather(x, (2 * lane) & 127, 1) + gather(x, (2 * lane + 1) & 127, 1)
        return gather(x, (2 * row) & 7, 0) + gather(x, (2 * row + 1) & 7, 0)

    def parted(halves):
        return [jnp.where(lane < 64, *(gather(halves[w][t], (2 * lane + h) & 127, 1) for w in (0, 1))) for t, h in PAIRS]

    def rows_of(ref, *index):
        return [[ref[(w, *index, pl.ds(t, 8, stride=2), slice(None))] for t in (0, 1)] for w in (0, 1)]

    def tiles(ref, *index):
        return [ref[(*index, q)] for q in range(4)]

    def put(ref, values, *index):
        for q, value in enumerate(values):
            ref[(*index, q)] = value

    for copy in bins_in:
        copy.wait()
    for j in range(8):
        halves = [[(1.0 - x.astype(F32) * 0.0625) ** 2 + 0.001 for x in half] for half in rows_of(bins_raw, j)]
        put(k0, parted(halves), 4 + j)
    for j in range(4):
        low, high = tiles(k0, 4 + 2 * j), tiles(k0, 5 + 2 * j)
        k1[5 + j] = 0.125 * (((low[0] + low[1]) + (low[2] + low[3])) + ((high[0] + high[1]) + (high[2] + high[3])))
    k2[6] = 0.125 * jnp.where(row < 4, halve_middle(k1[5] + k1[6]), halve_middle(k1[7] + k1[8]))
    for c in range(3):
        for copy in load_in[c]:
            copy.wait()
        for j in (0, 1, 6, 7, 2, 3, 4, 5):
            put(b0, parted(rows_of(load_raw, c, j)), c, 3 + j)

    pl.semaphore_wait(barrier, jnp.minimum(p, REACH_3) + jnp.minimum(n - 1 - p, REACH_3))
    start((*k0_all, *k1_all[:2], *k2_all[:6], *k1_all[2:], *b0_all[0], *b0_all[1], *b0_all[2], *outer_all, *k2_all[6:]))

    edges = (3 - 8 * p, 3 + 8 * (n - p))

    def x_face(f):
        inside = jnp.where(jnp.logical_or(f == edges[0], f == edges[1]), 0.0, 1.0)
        put(cx, [harmonic(first, second, 1.0) * inside for first, second in zip(tiles(k0, f), tiles(k0, f + 1))], f)

    def yz_faces(j):
        k = tiles(k0, j + 1)
        for ref, axis, last, (lows, highs) in ((cy, 0, row == 7, (k[0:2], k[2:4])), (cz, 1, lane == 127, (k[0::2], k[1::2]))):
            for i, (low, high) in enumerate(zip(lows, highs)):
                ref[j, i] = harmonic(low, high, 1.0)
                following = jnp.where(last, 0.0, harmonic(high, rolled(low, -1, axis), 1.0))
                ref[j, 2 + i] = following
                ref[j, 4 + i] = rolled(following, 1, axis)

    def diagonal(j):
        for q, (t, h) in enumerate(PAIRS):
            total = (mass_shift + (cx[j, q] + cx[j + 1, q])) + ((cy[j, h] + cy[j, 4 - 2 * t + h]) + (cz[j, t] + cz[j, 4 - 2 * h + t]))
            dg[j, q] = total
            inv = inverse(total)
            da[j, q] = inv * (1.0 / root_a)
            db[j, q] = inv * (1.0 / root_b)

    def fine_residue(b, v, before, after, j):
        result = []
        for q, (t, h) in enumerate(PAIRS):
            row_mate, lane_mate = v[2 * (1 - t) + h], v[2 * t + 1 - h]
            first = (cx[j, q] * before[q] + cx[j + 1, q] * after[q]) - dg[j, q] * v[q]
            if b is not None:
                first = first + b[q]
            second = cy[j, h] * row_mate + cy[j, 4 - 2 * t + h] * rolled(row_mate, 1 - 2 * t, 0)
            third = cz[j, t] * lane_mate + cz[j, 4 - 2 * h + t] * rolled(lane_mate, 1 - 2 * h, 1)
            result.append(first + (second + third))
        return result

    def first_v(c, j):
        v = [x * y for x, y in zip(tiles(b0, c, j), tiles(da, j))]
        put(v0, v, c, j)

    def second_v(c, j):
        v = tiles(v0, c, j)
        rest = fine_residue(tiles(b0, c, j), v, tiles(v0, c, j - 1), tiles(v0, c, j + 1), j)
        put(x0, [x + r * d for x, r, d in zip(v, rest, tiles(db, j))], c, j)

    def x_flux(c, f):
        flux = [cx[f, q] * (x0[c, f, q] - x0[c, f - 1, q]) for q in range(4)]
        return (flux[0] + flux[1]) + (flux[2] + flux[3])

    def block_sum(c, j):
        total, rows_up, lanes_up = [], [], []
        for i in (j, j + 1):
            b, x = tiles(b0, c, i), tiles(x0, c, i)
            total.append(((b[0] + b[1]) + (b[2] + b[3])) - mass_shift * ((x[0] + x[1]) + (x[2] + x[3])))
            for e in (0, 1):
                rows_up.append(cy[i, 2 + e] * (rolled(x[e], -1, 0) - x[2 + e]))
                lanes_up.append(cz[i, 2 + e] * (rolled(x[2 * e], -1, 1) - x[2 * e + 1]))
        rows_up = (rows_up[0] + rows_up[1]) + (rows_up[2] + rows_up[3])
        lanes_up = (lanes_up[0] + lanes_up[1]) + (lanes_up[2] + lanes_up[3])
        return (total[0] + total[1]) + ((rows_up - rolled(rows_up, 1, 0)) + (lanes_up - rolled(lanes_up, 1, 1)))

    for f in range(4, 11):
        x_face(f)
    for j in range(3, 11):
        yz_faces(j)
    for j in range(4, 10):
        diagonal(j)
    inner = []
    for c in range(3):
        for j in range(4, 10):
            first_v(c, j)
        for j in range(5, 9):
            second_v(c, j)
        middle = x_flux(c, 7)
        inner.append((block_sum(c, 5) + middle, block_sum(c, 7) - middle))

    receive(k0_all)
    for f in (1, 2, 3, 11, 12, 13):
        x_face(f)
    for j in (1, 2, 11, 12):
        yz_faces(j)
    for j in (1, 2, 3, 10, 11, 12):
        diagonal(j)

    def down(c):
        for j in (1, 2, 3, 10, 11, 12):
            first_v(c, j)
        for j in (2, 3, 4, 9, 10, 11):
            second_v(c, j)
        left, right = x_flux(c, 5), x_flux(c, 9)
        b1[c, 4] = 0.125 * (block_sum(c, 3) + (left - x_flux(c, 3)))
        b1[c, 5] = 0.125 * (inner[c][0] - left)
        b1[c, 6] = 0.125 * (inner[c][1] + right)
        b1[c, 7] = 0.125 * (block_sum(c, 9) + (x_flux(c, 11) - right))

    def edge_mask(count, spot, each):
        face = lax.broadcasted_iota(jnp.int32, (count, 8, 128), 0)
        return jnp.logical_or(face == spot - each * p, face == spot + each * (n - p))

    def level(k, count, spot, each, scale, hop, row_end, lane_end, x_ref, ref):
        x_ref[...] = jnp.where(edge_mask(count + 1, spot, each), 0.0, harmonic(k[:-1], k[1:], scale))
        faces = planar_faces(k[1:-1], scale, hop, row_end, lane_end)
        for i, face in enumerate(faces):
            ref[i] = face
        total = (mass_shift + (x_ref[:-1] + x_ref[1:])) + ((faces[0] + faces[1]) + (faces[2] + faces[3]))
        ref[4] = total
        inv = inverse(total)
        ref[5] = inv
        ref[6] = inv * (1.0 / root_a)
        ref[7] = inv * (1.0 / root_b)

    def apply(b, v, x_ref, ref, hop, first, last):
        inner = slice(first, last)
        coeffs = (x_ref[inner], x_ref[first + 1:last + 1], ref[0, inner], ref[1, inner], ref[2, inner], ref[3, inner], ref[4, inner])
        return residue(b, v[1:-1], v[:-2], v[2:], coeffs, hop)

    def widen(x, by):
        none = jnp.zeros((by, 8, 128), F32)
        return jnp.concatenate([none, x, none], axis=0)

    def pre_smooth(b, x_ref, ref):
        v = b * ref[6]
        return v[1:-1] + apply(b[1:-1], v, x_ref, ref, 1, 1, 11) * ref[7, 1:11]

    def post_smooth(b, start, x_ref, ref):
        v = start[1:-1] + apply(b[2:10], start, x_ref, ref, 1, 2, 10) * ref[7, 2:10]
        return v[1:-1] + apply(b[3:9], v, x_ref, ref, 1, 3, 9) * ref[6, 3:9]

    def share(b, x_ref, ref):
        v = widen(b * ref[6, 4:8], 2)
        x = widen(v[1:-1] + apply(widen(b, 1), v, x_ref, ref, 1, 3, 9) * ref[7, 3:9], 2)
        return apply(widen(b, 2), x, x_ref, ref, 1, 2, 10)

    receive(k1_all)
    level(k1[...], 12, 4, 4, 0.25, 1, (row == 7)[None], (lane == 127)[None], c1x, c1)
    receive(k2_all[:6])
    near = k2[3:10]
    turned = rolled(near, 4, 1)
    near = jnp.stack([jnp.where(row < 4, near, turned), jnp.where(row < 4, turned, near)], axis=1).reshape(14, 8, 128)
    level(near, 12, 5, 2, 0.25 ** 2, 1, ((row & 3) == 3)[None], ((lane & 63) == 63)[None], c2x, c2)

    rest = []
    for c in range(3):
        receive(b0_all[c])
        down(c)
        if c > 0:
            rest.append(share(b1[c - 1, 4:8], c1x, c1))
        start(b1_all[c])
    rest.append(share(b1[2, 4:8], c1x, c1))
    quarter = (row >= 4).astype(jnp.int32) * 2 + (lane >= 64).astype(jnp.int32)
    for j in range(4):
        parts = [halve_middle(r[2 * j] + r[2 * j + 1]) for r in rest]
        m2[3, j] = 0.125 * jnp.where(quarter == 0, parts[0], jnp.where(quarter == 1, parts[1], jnp.where(quarter == 2, parts[2], 0.0)))

    start(m2_all)

    def halve_coarse(first, second):
        x = first + second
        x = x + gather(x, jnp.broadcast_to((row ^ 1)[None], x.shape), 1)
        return 0.125 * (x + gather(x, jnp.broadcast_to((lane ^ 1)[None], x.shape), 2))

    rest = widen(share(m2[3], c2x, c2), 1).reshape(5, 2, 8, 128)
    low = halve_coarse(rest[:, 0], rest[:, 1])
    odd_row, odd_lane = (row & 1) == 1, (lane & 1) == 1
    four = jnp.where(odd_row, jnp.where(odd_lane, low[3], low[2]), jnp.where(odd_lane, low[1], low[0]))
    last = rolled(low[4], 64, 1)
    last = jnp.where(odd_row, last, rolled(jnp.where(odd_lane, low[4], last), 4, 0))
    m3[7] = jnp.where(quarter == 3, last, four)
    start(m3_all)

    receive(k2_all[6:])
    level(halve_coarse(k2[...], rolled(k2[...], 4, 1)), 11, 5, 1, 0.25 ** 3, 2, ((row & 3) >= 2)[None], ((lane & 63) >= 62)[None], c3x, c3)

    receive(outer_all)
    for f in (0, 14):
        x_face(f)
    for j in (0, 13):
        yz_faces(j)
        diagonal(j)
    for c in range(3):
        for j in (0, 13):
            first_v(c, j)
        for j in (1, 12):
            second_v(c, j)

    smooth_1 = []
    for c in range(3):
        receive(b1_all[c])
        smooth_1.append(pre_smooth(b1[c], c1x, c1))
    for c in range(3):
        half_way = {}
        for j in range(2, 12):
            x = tiles(x0, c, j)
            rest = fine_residue(tiles(b0, c, j), x, tiles(x0, c, j - 1), tiles(x0, c, j + 1), j)
            half_way[j] = [x + r * d for x, r, d in zip(x, rest, tiles(db, j))]
            if j >= 4:
                i = j - 1
                rest = fine_residue(tiles(b0, c, i), half_way[i], half_way[i - 1], half_way[i + 1], i)
                put(v0, [x + r * d for x, r, d in zip(half_way[i], rest, tiles(da, i))], c, i)

    receive(m2_all)
    b2 = jnp.stack([m2[3 + i // 2, 1] + m2[2 + i // 2, 3] if i % 2 == 0 else m2[3 + i // 2, 2] + m2[4 + i // 2, 0]
                    for i in range(-5, 7)])
    smooth_2 = pre_smooth(b2, c2x, c2)

    receive(m3_all)
    packed = m3[...]

    def spots(index, count):
        return jnp.broadcast_to(index[None], (count, 8, 128))

    left, right = gather(packed, spots(lane & 126, 15), 2), gather(packed, spots(lane | 1, 15), 2)
    upper, lower = left[4:15] + right[3:14], left[2:13] + right[1:12]
    last = gather(packed[0:11], spots(jnp.where(lane < 64, 64 + (lane & 126), lane | 1), 11), 2)
    last = gather(last, spots(jnp.where(row < 4, 4 + (row & 6), row | 1), 11), 1)
    b3 = gather(upper, spots(row & 6, 11), 1) + gather(lower, spots(row | 1, 11), 1) + last
    low = b3 * (c3[5] * (1.0 / bottom_roots[0]))
    for i in (1, 2, 3):
        inner = slice(i, 11 - i)
        low = low[1:-1] + apply(b3[inner], low, c3x, c3, 2, i, 11 - i) * (c3[5, inner] * (1.0 / bottom_roots[i]))
    v = smooth_2 + jnp.broadcast_to(low[:, None], (5, 2, 8, 128)).reshape(10, 8, 128)
    x = post_smooth(b2, v, c2x, c2)

    ups = []
    for c in range(3):
        spread = []
        for j in range(6):
            half = gather(x[j], 64 * (c % 2) + (lane >> 1), 1)
            spread.append(gather(half, 4 * (c // 2) + (row >> 1), 0))
        v = smooth_1[c] + jnp.stack([spread[(i + 1) // 2] for i in range(10)])
        ups.append(post_smooth(b1[c], v, c1x, c1))

    for c in range(3):
        coarse = ups[c]
        rows_by = [[rolled(e, 1 - 2 * t, 0) - e for t in (0, 1)] for e in coarse]
        lanes_by = [[rolled(e, 1 - 2 * h, 1) - e for h in (0, 1)] for e in coarse]
        half_way = {}
        for j in range(2, 12):
            own, upper = (j - 1) // 2, 1 - j % 2
            e, step = coarse[own], coarse[own + 2 * upper - 1] - coarse[own]
            half_way[j] = []
            for q, (t, h) in enumerate(PAIRS):
                flux = (cx[j + upper, q] * step + cy[j, 4 - 2 * t + h] * rows_by[own][t]) + (
                    cz[j, 4 - 2 * h + t] * lanes_by[own][h] - mass_shift * e)
                half_way[j].append(e + db[j, q] * flux)
            if j >= 4:
                i = j - 1
                rest = fine_residue(None, half_way[i], half_way[i - 1], half_way[i + 1], i)
                done = [y + (x + r * d) for y, x, r, d in zip(tiles(v0, c, i), half_way[i], rest, tiles(da, i))]
                slot = 8 * c + i - 3
                for w in (0, 1):
                    for t in (0, 1):
                        left, right = (x if h == w else rolled(x, 64, 1) for h, x in enumerate(done[2 * t:2 * t + 2]))
                        tmp[slot, w, pl.ds(t, 8, stride=2), :] = gather(jnp.where(lane < 64, left, right), (lane >> 1) + 64 * (lane & 1), 1)
                    out_ref[c, i - 3, :, 128 * w:128 * w + 128] = tmp[slot, w]
    finish(early + late)


def solution(mesh):
    wide, grp = mesh.shape["wide"], mesh.shape["grp"]

    def on_device(load, bins):
        def plane(*lead):
            return pltpu.VMEM((*lead, 4, 8, 128), F32)

        def small(*lead):
            return pltpu.VMEM((*lead, 8, 128), F32)

        return pl.pallas_call(
            functools.partial(kernel, wide * grp, wide, grp),
            out_shape=pltpu.VMEM(load.shape, F32),
            in_specs=[pl.BlockSpec(memory_space=pl.ANY)] * 2,
            out_specs=pl.BlockSpec(memory_space=pltpu.VMEM),
            scratch_shapes=[
                pltpu.VMEM((2, 3, 8, 16, 128), F32), pltpu.VMEM((2, 8, 16, 128), jnp.int32),
                plane(3, 14), plane(16), plane(15), small(14, 6), small(14, 6), plane(14), plane(14), plane(14),
                plane(3, 14), plane(3, 14), pltpu.VMEM((24, 2, 16, 128), F32),
                small(3, 12), small(14), small(13), small(8, 12),
                small(13), small(7, 4), small(13), small(8, 12),
                small(15), small(12), small(8, 11),
                pltpu.SemaphoreType.DMA((REMOTE,)), pltpu.SemaphoreType.DMA((REMOTE,)), pltpu.SemaphoreType.DMA((8,)),
            ],
            compiler_params=pltpu.CompilerParams(
                collective_id=0, has_side_effects=True, vmem_limit_bytes=60 * 1024 * 1024),
        )(load, bins)

    return jax.shard_map(
        on_device,
        mesh=mesh,
        in_specs=(P(None, ("wide", "grp"), None, None), P(("wide", "grp"), None, None)),
        out_specs=P(None, ("wide", "grp"), None, None),
        check_vma=False,
    )
```

```python
import functools
import itertools
import math

import jax
import jax.numpy as jnp
from jax import lax
from jax.experimental import pallas as pl
from jax.experimental.pallas import tpu as pltpu
from jax.sharding import PartitionSpec as P

MESH = pl.DeviceIdType.MESH
F32 = jnp.float32

mass_shift = 0.1
root_a = 1.15 + 0.85 * math.sqrt(0.5)
root_b = 1.15 - 0.85 * math.sqrt(0.5)
bottom_roots = (
    1.1 + 0.9 * math.cos(math.pi / 8),
    1.1 - 0.9 * math.cos(math.pi / 8),
    1.1 + 0.9 * math.cos(3 * math.pi / 8),
    1.1 - 0.9 * math.cos(3 * math.pi / 8),
)

REMOTE = 54
REACH_K, REACH_2, REACH_3 = 6, 3, 7
PAIRS = ((0, 0), (0, 1), (1, 0), (1, 1))


def inverse(x):
    guess = pltpu.reciprocal(x, approx=True)
    return guess * (2.0 - x * guess)


def harmonic(first, second, scale):
    return (2.0 * scale) * (first * second) * inverse(first + second)


def gather(x, index, axis):
    return jnp.take_along_axis(x, index, axis=axis, mode="promise_in_bounds")


def rolled(x, shift, axis):
    return pltpu.roll(x, shift % x.shape[axis], axis)


def planar_faces(k, scale, hop, row_end, lane_end):
    axis = k.ndim - 2
    rows_up = jnp.where(row_end, 0.0, harmonic(k, rolled(k, -hop, axis), scale))
    lanes_up = jnp.where(lane_end, 0.0, harmonic(k, rolled(k, -hop, axis + 1), scale))
    return rows_up, rolled(rows_up, hop, axis), lanes_up, rolled(lanes_up, hop, axis + 1)


def residue(b, v, before, after, c, hop):
    axis = v.ndim - 2
    first = (b - c[6] * v) + (c[0] * before + c[1] * after)
    second = c[2] * rolled(v, -hop, axis) + c[3] * rolled(v, hop, axis)
    third = c[4] * rolled(v, -hop, axis + 1) + c[5] * rolled(v, hop, axis + 1)
    return first + (second + third)


def kernel(n, wide, grp, load_ref, bins_ref, out_ref, load_raw, bins_raw, b0, k0, cx, cy, cz, dg, da, db,
           v0, x0, tmp, b1, k1, c1x, c1, k2, m2, c2x, c2, m3, c3x, c3, send, recv, local):
    p = lax.axis_index("wide") * grp + lax.axis_index("grp")
    numbers = iter(range(REMOTE))

    def place(distance):
        spot = lax.axis_index("grp") + distance
        if distance > 0:
            carry = jnp.where(spot >= grp, 1, 0)
        else:
            carry = jnp.where(spot < 0, -1, 0)
        return {"wide": lax.axis_index("wide") + carry, "grp": spot - carry * grp}

    def there(distance):
        return p + distance < n if distance > 0 else p + distance >= 0

    class Message:
        def __init__(self, src, dst, distance):
            number = next(numbers)
            self.distance = distance
            self.copy = pltpu.make_async_remote_copy(
                src_ref=src, dst_ref=dst, send_sem=send.at[number], recv_sem=recv.at[number],
                device_id=place(distance), device_id_type=MESH)

    def both_ways(reach):
        return [d for step in range(1, reach + 1) for d in (step, -step)]

    k0_all = [Message(k0.at[9:12], k0.at[1:4], 1), Message(k0.at[4:7], k0.at[12:15], -1)]
    b0_all = [(Message(b0.at[c, 9:11], b0.at[c, 1:3], 1), Message(b0.at[c, 3:5], b0.at[c, 11:13], -1)) for c in range(3)]
    k1_all = [Message(k1.at[5:9], k1.at[1:5], 1), Message(k1.at[5:9], k1.at[9:13], -1),
              Message(k1.at[8], k1.at[0], 2), Message(k1.at[5], k1.at[13], -2)]
    b1_all = [(Message(b1.at[c, 4:8], b1.at[c, 0:4], 1), Message(b1.at[c, 4:8], b1.at[c, 8:12], -1)) for c in range(3)]
    outer_all = [Message(k0.at[8], k0.at[0], 1), Message(k0.at[7], k0.at[15], -1),
                 Message(b0.at[:, 8], b0.at[:, 0], 1), Message(b0.at[:, 5], b0.at[:, 13], -1)]
    k2_all = [Message(k2.at[6], k2.at[6 - d], d) for d in both_ways(REACH_K)]
    part = {3: slice(2, 4), -3: slice(0, 2)}
    m2_all = [Message(m2.at[3, part.get(d, slice(0, 4))], m2.at[3 - d, part.get(d, slice(0, 4))], d) for d in both_ways(REACH_2)]
    m3_all = [Message(m3.at[7], m3.at[7 - d], d) for d in both_ways(REACH_3)]
    early = [*outer_all, *k0_all, *b0_all[0], *b0_all[1], *b0_all[2], *k1_all, *k2_all, *b1_all[0], *b1_all[1], *b1_all[2]]
    late = [*m3_all, *m2_all]

    def grouped(messages, sign, act):
        for distance, run in itertools.groupby(messages, lambda m: sign * m.distance):
            run = list(run)

            @pl.when(there(distance))
            def _():
                for m in run:
                    act(m.copy)

    def start(messages):
        grouped(messages, 1, lambda copy: copy.start())

    def finish(messages):
        grouped(sorted(messages, key=lambda m: m.distance), 1, lambda copy: copy.wait_send())

    def receive(messages):
        grouped(sorted(messages, key=lambda m: m.distance), -1, lambda copy: copy.wait_recv())

    @pl.when(jnp.logical_or(p < REACH_3, p >= n - REACH_3))
    def _():
        for halo in (slice(0, 4), slice(12, 16)):
            k0[halo] = jnp.ones((4, 4, 8, 128), F32)
        for halo in (slice(0, 3), slice(11, 14)):
            b0[:, halo] = jnp.zeros((3, 3, 4, 8, 128), F32)
        k1[...] = jnp.ones_like(k1)
        b1[...] = jnp.zeros_like(b1)
        k2[...] = jnp.ones_like(k2)
        m2[...] = jnp.zeros_like(m2)
        m3[...] = jnp.zeros_like(m3)

    barrier = pltpu.get_barrier_semaphore()
    for d in both_ways(REACH_3):
        pl.when(there(d))(functools.partial(
            pl.semaphore_signal, barrier, inc=1, device_id=place(d), device_id_type=MESH))

    bins_in = [pltpu.make_async_copy(bins_ref.at[:, :, 128 * w:128 * w + 128], bins_raw.at[w], local.at[w]) for w in (0, 1)]
    load_in = [[pltpu.make_async_copy(load_ref.at[c, :, :, 128 * w:128 * w + 128], load_raw.at[w, c], local.at[2 + 2 * c + w])
                for w in (0, 1)] for c in range(3)]
    for copy in (*bins_in, *load_in[0], *load_in[1], *load_in[2]):
        copy.start()
    row = lax.broadcasted_iota(jnp.int32, (8, 128), 0)
    lane = lax.broadcasted_iota(jnp.int32, (8, 128), 1)

    def halve_middle(x):
        x = gather(x, (2 * lane) & 127, 1) + gather(x, (2 * lane + 1) & 127, 1)
        return gather(x, (2 * row) & 7, 0) + gather(x, (2 * row + 1) & 7, 0)

    def parted(halves):
        return [jnp.where(lane < 64, *(gather(halves[w][t], (2 * lane + h) & 127, 1) for w in (0, 1))) for t, h in PAIRS]

    def rows_of(ref, *index):
        return [[ref[(w, *index, pl.ds(t, 8, stride=2), slice(None))] for t in (0, 1)] for w in (0, 1)]

    def tiles(ref, *index):
        return [ref[(*index, q)] for q in range(4)]

    def put(ref, values, *index):
        for q, value in enumerate(values):
            ref[(*index, q)] = value

    for copy in bins_in:
        copy.wait()
    for j in range(8):
        halves = [[(1.0 - x.astype(F32) * 0.0625) ** 2 + 0.001 for x in half] for half in rows_of(bins_raw, j)]
        put(k0, parted(halves), 4 + j)
    for j in range(4):
        low, high = tiles(k0, 4 + 2 * j), tiles(k0, 5 + 2 * j)
        k1[5 + j] = 0.125 * (((low[0] + low[1]) + (low[2] + low[3])) + ((high[0] + high[1]) + (high[2] + high[3])))
    k2[6] = 0.125 * jnp.where(row < 4, halve_middle(k1[5] + k1[6]), halve_middle(k1[7] + k1[8]))
    for c in range(3):
        for copy in load_in[c]:
            copy.wait()
        for j in (0, 1, 6, 7, 2, 3, 4, 5):
            put(b0, parted(rows_of(load_raw, c, j)), c, 3 + j)

    pl.semaphore_wait(barrier, jnp.minimum(p, REACH_3) + jnp.minimum(n - 1 - p, REACH_3))
    start((*k0_all, *k1_all[:2], *k2_all[:6], *k1_all[2:], *b0_all[0], *b0_all[1], *b0_all[2], *outer_all, *k2_all[6:]))

    edges = (3 - 8 * p, 3 + 8 * (n - p))

    def x_face(f):
        inside = jnp.where(jnp.logical_or(f == edges[0], f == edges[1]), 0.0, 1.0)
        put(cx, [harmonic(first, second, 1.0) * inside for first, second in zip(tiles(k0, f), tiles(k0, f + 1))], f)

    def yz_faces(j):
        k = tiles(k0, j + 1)
        for ref, axis, last, (lows, highs) in ((cy, 0, row == 7, (k[0:2], k[2:4])), (cz, 1, lane == 127, (k[0::2], k[1::2]))):
            for i, (low, high) in enumerate(zip(lows, highs)):
                ref[j, i] = harmonic(low, high, 1.0)
                following = jnp.where(last, 0.0, harmonic(high, rolled(low, -1, axis), 1.0))
                ref[j, 2 + i] = following
                ref[j, 4 + i] = rolled(following, 1, axis)

    def diagonal(j):
        for q, (t, h) in enumerate(PAIRS):
            total = (mass_shift + (cx[j, q] + cx[j + 1, q])) + ((cy[j, h] + cy[j, 4 - 2 * t + h]) + (cz[j, t] + cz[j, 4 - 2 * h + t]))
            dg[j, q] = total
            inv = inverse(total)
            da[j, q] = inv * (1.0 / root_a)
            db[j, q] = inv * (1.0 / root_b)

    def fine_residue(b, v, before, after, j):
        result = []
        for q, (t, h) in enumerate(PAIRS):
            row_mate, lane_mate = v[2 * (1 - t) + h], v[2 * t + 1 - h]
            first = (cx[j, q] * before[q] + cx[j + 1, q] * after[q]) - dg[j, q] * v[q]
            if b is not None:
                first = first + b[q]
            second = cy[j, h] * row_mate + cy[j, 4 - 2 * t + h] * rolled(row_mate, 1 - 2 * t, 0)
            third = cz[j, t] * lane_mate + cz[j, 4 - 2 * h + t] * rolled(lane_mate, 1 - 2 * h, 1)
            result.append(first + (second + third))
        return result

    def first_v(c, j):
        v = [x * y for x, y in zip(tiles(b0, c, j), tiles(da, j))]
        put(v0, v, c, j)

    def second_v(c, j):
        v = tiles(v0, c, j)
        rest = fine_residue(tiles(b0, c, j), v, tiles(v0, c, j - 1), tiles(v0, c, j + 1), j)
        put(x0, [x + r * d for x, r, d in zip(v, rest, tiles(db, j))], c, j)

    def x_flux(c, f):
        flux = [cx[f, q] * (x0[c, f, q] - x0[c, f - 1, q]) for q in range(4)]
        return (flux[0] + flux[1]) + (flux[2] + flux[3])

    def block_sum(c, j):
        total, rows_up, lanes_up = [], [], []
        for i in (j, j + 1):
            b, x = tiles(b0, c, i), tiles(x0, c, i)
            total.append(((b[0] + b[1]) + (b[2] + b[3])) - mass_shift * ((x[0] + x[1]) + (x[2] + x[3])))
            for e in (0, 1):
                rows_up.append(cy[i, 2 + e] * (rolled(x[e], -1, 0) - x[2 + e]))
                lanes_up.append(cz[i, 2 + e] * (rolled(x[2 * e], -1, 1) - x[2 * e + 1]))
        rows_up = (rows_up[0] + rows_up[1]) + (rows_up[2] + rows_up[3])
        lanes_up = (lanes_up[0] + lanes_up[1]) + (lanes_up[2] + lanes_up[3])
        return (total[0] + total[1]) + ((rows_up - rolled(rows_up, 1, 0)) + (lanes_up - rolled(lanes_up, 1, 1)))

    for f in range(4, 11):
        x_face(f)
    for j in range(3, 11):
        yz_faces(j)
    for j in range(4, 10):
        diagonal(j)
    inner = []
    for c in range(3):
        for j in range(4, 10):
            first_v(c, j)
        for j in range(5, 9):
            second_v(c, j)
        middle = x_flux(c, 7)
        inner.append((block_sum(c, 5) + middle, block_sum(c, 7) - middle))

    receive(k0_all)
    for f in (1, 2, 3, 11, 12, 13):
        x_face(f)
    for j in (1, 2, 11, 12):
        yz_faces(j)
    for j in (1, 2, 3, 10, 11, 12):
        diagonal(j)

    def down(c):
        for j in (1, 2, 3, 10, 11, 12):
            first_v(c, j)
        for j in (2, 3, 4, 9, 10, 11):
            second_v(c, j)
        left, right = x_flux(c, 5), x_flux(c, 9)
        b1[c, 4] = 0.125 * (block_sum(c, 3) + (left - x_flux(c, 3)))
        b1[c, 5] = 0.125 * (inner[c][0] - left)
        b1[c, 6] = 0.125 * (inner[c][1] + right)
        b1[c, 7] = 0.125 * (block_sum(c, 9) + (x_flux(c, 11) - right))

    def edge_mask(count, spot, each):
        face = lax.broadcasted_iota(jnp.int32, (count, 8, 128), 0)
        return jnp.logical_or(face == spot - each * p, face == spot + each * (n - p))

    def level(k, count, spot, each, scale, hop, row_end, lane_end, x_ref, ref):
        x_ref[...] = jnp.where(edge_mask(count + 1, spot, each), 0.0, harmonic(k[:-1], k[1:], scale))
        faces = planar_faces(k[1:-1], scale, hop, row_end, lane_end)
        for i, face in enumerate(faces):
            ref[i] = face
        total = (mass_shift + (x_ref[:-1] + x_ref[1:])) + ((faces[0] + faces[1]) + (faces[2] + faces[3]))
        ref[4] = total
        inv = inverse(total)
        ref[5] = inv
        ref[6] = inv * (1.0 / root_a)
        ref[7] = inv * (1.0 / root_b)

    def apply(b, v, x_ref, ref, hop, first, last):
        inner = slice(first, last)
        coeffs = (x_ref[inner], x_ref[first + 1:last + 1], ref[0, inner], ref[1, inner], ref[2, inner], ref[3, inner], ref[4, inner])
        return residue(b, v[1:-1], v[:-2], v[2:], coeffs, hop)

    def widen(x, by):
        none = jnp.zeros((by, 8, 128), F32)
        return jnp.concatenate([none, x, none], axis=0)

    def pre_smooth(b, x_ref, ref):
        v = b * ref[6]
        return v[1:-1] + apply(b[1:-1], v, x_ref, ref, 1, 1, 11) * ref[7, 1:11]

    def post_smooth(b, start, x_ref, ref):
        v = start[1:-1] + apply(b[2:10], start, x_ref, ref, 1, 2, 10) * ref[7, 2:10]
        return v[1:-1] + apply(b[3:9], v, x_ref, ref, 1, 3, 9) * ref[6, 3:9]

    def share(b, x_ref, ref):
        v = widen(b * ref[6, 4:8], 2)
        x = widen(v[1:-1] + apply(widen(b, 1), v, x_ref, ref, 1, 3, 9) * ref[7, 3:9], 2)
        return apply(widen(b, 2), x, x_ref, ref, 1, 2, 10)

    receive(k1_all)
    level(k1[...], 12, 4, 4, 0.25, 1, (row == 7)[None], (lane == 127)[None], c1x, c1)
    receive(k2_all[:6])
    near = k2[3:10]
    turned = rolled(near, 4, 1)
    near = jnp.stack([jnp.where(row < 4, near, turned), jnp.where(row < 4, turned, near)], axis=1).reshape(14, 8, 128)
    level(near, 12, 5, 2, 0.25 ** 2, 1, ((row & 3) == 3)[None], ((lane & 63) == 63)[None], c2x, c2)

    rest = []
    for c in range(3):
        receive(b0_all[c])
        down(c)
        if c > 0:
            rest.append(share(b1[c - 1, 4:8], c1x, c1))
        start(b1_all[c])
    rest.append(share(b1[2, 4:8], c1x, c1))
    quarter = (row >= 4).astype(jnp.int32) * 2 + (lane >= 64).astype(jnp.int32)
    for j in range(4):
        parts = [halve_middle(r[2 * j] + r[2 * j + 1]) for r in rest]
        m2[3, j] = 0.125 * jnp.where(quarter == 0, parts[0], jnp.where(quarter == 1, parts[1], jnp.where(quarter == 2, parts[2], 0.0)))

    start(m2_all)

    def halve_coarse(first, second):
        x = first + second
        x = x + gather(x, jnp.broadcast_to((row ^ 1)[None], x.shape), 1)
        return 0.125 * (x + gather(x, jnp.broadcast_to((lane ^ 1)[None], x.shape), 2))

    rest = widen(share(m2[3], c2x, c2), 1).reshape(5, 2, 8, 128)
    low = halve_coarse(rest[:, 0], rest[:, 1])
    odd_row, odd_lane = (row & 1) == 1, (lane & 1) == 1
    four = jnp.where(odd_row, jnp.where(odd_lane, low[3], low[2]), jnp.where(odd_lane, low[1], low[0]))
    last = rolled(low[4], 64, 1)
    last = jnp.where(odd_row, last, rolled(jnp.where(odd_lane, low[4], last), 4, 0))
    m3[7] = jnp.where(quarter == 3, last, four)
    start(m3_all)

    receive(k2_all[6:])
    level(halve_coarse(k2[...], rolled(k2[...], 4, 1)), 11, 5, 1, 0.25 ** 3, 2, ((row & 3) >= 2)[None], ((lane & 63) >= 62)[None], c3x, c3)

    receive(outer_all)
    for f in (0, 14):
        x_face(f)
    for j in (0, 13):
        yz_faces(j)
        diagonal(j)
    for c in range(3):
        for j in (0, 13):
            first_v(c, j)
        for j in (1, 12):
            second_v(c, j)

    smooth_1 = []
    for c in range(3):
        receive(b1_all[c])
        smooth_1.append(pre_smooth(b1[c], c1x, c1))
    for c in range(3):
        half_way = {}
        for j in range(2, 12):
            x = tiles(x0, c, j)
            rest = fine_residue(tiles(b0, c, j), x, tiles(x0, c, j - 1), tiles(x0, c, j + 1), j)
            half_way[j] = [x + r * d for x, r, d in zip(x, rest, tiles(db, j))]
            if j >= 4:
                i = j - 1
                rest = fine_residue(tiles(b0, c, i), half_way[i], half_way[i - 1], half_way[i + 1], i)
                put(v0, [x + r * d for x, r, d in zip(half_way[i], rest, tiles(da, i))], c, i)

    receive(m2_all)
    b2 = jnp.stack([m2[3 + i // 2, 1] + m2[2 + i // 2, 3] if i % 2 == 0 else m2[3 + i // 2, 2] + m2[4 + i // 2, 0]
                    for i in range(-5, 7)])
    smooth_2 = pre_smooth(b2, c2x, c2)

    finish(early)
    receive(m3_all)
    packed = m3[...]

    def spots(index, count):
        return jnp.broadcast_to(index[None], (count, 8, 128))

    left, right = gather(packed, spots(lane & 126, 15), 2), gather(packed, spots(lane | 1, 15), 2)
    upper, lower = left[4:15] + right[3:14], left[2:13] + right[1:12]
    last = gather(packed[0:11], spots(jnp.where(lane < 64, 64 + (lane & 126), lane | 1), 11), 2)
    last = gather(last, spots(jnp.where(row < 4, 4 + (row & 6), row | 1), 11), 1)
    b3 = gather(upper, spots(row & 6, 11), 1) + gather(lower, spots(row | 1, 11), 1) + last
    low = b3 * (c3[5] * (1.0 / bottom_roots[0]))
    for i in (1, 2, 3):
        inner = slice(i, 11 - i)
        low = low[1:-1] + apply(b3[inner], low, c3x, c3, 2, i, 11 - i) * (c3[5, inner] * (1.0 / bottom_roots[i]))
    v = smooth_2 + jnp.broadcast_to(low[:, None], (5, 2, 8, 128)).reshape(10, 8, 128)
    x = post_smooth(b2, v, c2x, c2)

    ups = []
    for c in range(3):
        spread = []
        for j in range(6):
            half = gather(x[j], 64 * (c % 2) + (lane >> 1), 1)
            spread.append(gather(half, 4 * (c // 2) + (row >> 1), 0))
        v = smooth_1[c] + jnp.stack([spread[(i + 1) // 2] for i in range(10)])
        ups.append(post_smooth(b1[c], v, c1x, c1))

    for c in range(3):
        coarse = ups[c]
        rows_by = [[rolled(e, 1 - 2 * t, 0) - e for t in (0, 1)] for e in coarse]
        lanes_by = [[rolled(e, 1 - 2 * h, 1) - e for h in (0, 1)] for e in coarse]
        half_way = {}
        for j in range(2, 12):
            own, upper = (j - 1) // 2, 1 - j % 2
            e, step = coarse[own], coarse[own + 2 * upper - 1] - coarse[own]
            half_way[j] = []
            for q, (t, h) in enumerate(PAIRS):
                flux = (cx[j + upper, q] * step + cy[j, 4 - 2 * t + h] * rows_by[own][t]) + (
                    cz[j, 4 - 2 * h + t] * lanes_by[own][h] - mass_shift * e)
                half_way[j].append(e + db[j, q] * flux)
            if j >= 4:
                i = j - 1
                rest = fine_residue(None, half_way[i], half_way[i - 1], half_way[i + 1], i)
                done = [y + (x + r * d) for y, x, r, d in zip(tiles(v0, c, i), half_way[i], rest, tiles(da, i))]
                slot = 8 * c + i - 3
                for w in (0, 1):
                    for t in (0, 1):
                        left, right = (x if h == w else rolled(x, 64, 1) for h, x in enumerate(done[2 * t:2 * t + 2]))
                        tmp[slot, w, pl.ds(t, 8, stride=2), :] = gather(jnp.where(lane < 64, left, right), (lane >> 1) + 64 * (lane & 1), 1)
                    out_ref[c, i - 3, :, 128 * w:128 * w + 128] = tmp[slot, w]
    finish(late)


def solution(mesh):
    wide, grp = mesh.shape["wide"], mesh.shape["grp"]

    def on_device(load, bins):
        def plane(*lead):
            return pltpu.VMEM((*lead, 4, 8, 128), F32)

        def small(*lead):
            return pltpu.VMEM((*lead, 8, 128), F32)

        return pl.pallas_call(
            functools.partial(kernel, wide * grp, wide, grp),
            out_shape=pltpu.VMEM(load.shape, F32),
            in_specs=[pl.BlockSpec(memory_space=pl.ANY)] * 2,
            out_specs=pl.BlockSpec(memory_space=pltpu.VMEM),
            scratch_shapes=[
                pltpu.VMEM((2, 3, 8, 16, 128), F32), pltpu.VMEM((2, 8, 16, 128), jnp.int32),
                plane(3, 14), plane(16), plane(15), small(14, 6), small(14, 6), plane(14), plane(14), plane(14),
                plane(3, 14), plane(3, 14), pltpu.VMEM((24, 2, 16, 128), F32),
                small(3, 12), small(14), small(13), small(8, 12),
                small(13), small(7, 4), small(13), small(8, 12),
                small(15), small(12), small(8, 11),
                pltpu.SemaphoreType.DMA((REMOTE,)), pltpu.SemaphoreType.DMA((REMOTE,)), pltpu.SemaphoreType.DMA((8,)),
            ],
            compiler_params=pltpu.CompilerParams(
                collective_id=0, has_side_effects=True, vmem_limit_bytes=60 * 1024 * 1024),
        )(load, bins)

    return jax.shard_map(
        on_device,
        mesh=mesh,
        in_specs=(P(None, ("wide", "grp"), None, None), P(("wide", "grp"), None, None)),
        out_specs=P(None, ("wide", "grp"), None, None),
        check_vma=False,
    )
```
